32 devices in a mesh: fsdp: 8 (over z, y), tensor: 4 (over x, core).
Axes of the slice: x: 2, y: 2, z: 4, core: 2. Of those that a mesh axis runs over, the one named last changes fastest.
Arguments:
- layer_input: bfloat16 [2048, 8192], P('fsdp', 'tensor'), may hold values from -6 to 6
- value_grad: bfloat16 [2048, 1024], P('fsdp', 'tensor'), may hold values from -6 to 6
- quant_codes: int32 [8192, 1024], P('fsdp', 'tensor'), may hold values from 0 to 15
- block_scales: float32 [8192, 16], P('fsdp', 'tensor'), may hold values from 0.02 to 0.08
- tenant_ids: int32 [128], P('fsdp'), may hold values from 0 to 7
- live_counts: int32 [8], P('fsdp'), may hold values from 12 to 16, as said below
- tenant_owner: int32 [8], replicated, may hold values from 0 to 7, each once
- factor_down: float32 [8, 16, 8192], P('fsdp', None, 'tensor'), may hold values from -6 to 6
- factor_up: float32 [8, 16, 1024], P('fsdp', None, 'tensor'), may hold values from -6 to 6
- moment_down: float32 [8, 16, 8192], P('fsdp', None, 'tensor'), may hold values from -6 to 6
- second_down: float32 [8, 16, 8192], P('fsdp', None, 'tensor'), may hold values from 0.05 to 5
- moment_up: float32 [8, 16, 1024], P('fsdp', None, 'tensor'), may hold values from -6 to 6
- second_up: float32 [8, 16, 1024], P('fsdp', None, 'tensor'), may hold values from 0.05 to 5
Outputs:
- layer_input_gradient: bfloat16 [2048, 8192], P('fsdp', 'tensor')
- new_down: float32 [8, 16, 8192], P('fsdp', None, 'tensor')
- new_up: float32 [8, 16, 1024], P('fsdp', None, 'tensor')
- new_moment_down: float32 [8, 16, 8192], P('fsdp', None, 'tensor')
- new_second_down: float32 [8, 16, 8192], P('fsdp', None, 'tensor')
- new_moment_up: float32 [8, 16, 1024], P('fsdp', None, 'tensor')
- new_second_up: float32 [8, 16, 1024], P('fsdp', None, 'tensor')
The draws below stay inside these ranges and needn't reach their ends.
Inputs may be any that keep to these rules, and one draw needn't show every extreme that they name: The first live_counts[f] sequence slots of fsdp index f are live and the rest are padding; some index has all 16 live. tenant_owner is a permutation: tenant t's adapter and its moments sit in slot tenant_owner[t].
All inputs are finite; a program needn't handle non-finite values.
Results may differ from the reference program's by a relative error of at most 0.01.
Values may be sent and summed in bfloat16 or wider, within the bound.
A program may use at most 128 MiB of HBM per device.

```python
import math
import jax
import jax.numpy as jnp
from jax import lax

MODEL_WIDTH = 8192
ADAPTER_RANK = 16
QB = 64
SEQ = 16
SLOTS = 16
KV = 1024
TENANTS = 8
TOKEN_TOTAL = 2048
N_FSDP = 8


def draw_live_counts(key, part):
    counts = jax.random.randint(key, (N_FSDP,), SLOTS * 3 // 4, SLOTS + 1, dtype=jnp.int32)
    chosen = jax.random.randint(jax.random.fold_in(key, 7), (), 0, N_FSDP, dtype=jnp.int32)
    filled = jnp.where(jnp.arange(N_FSDP, dtype=jnp.int32) == chosen, SLOTS, counts)
    return filled.astype(jnp.int32)


def place_ends(entries, rng, low, high):
    dims = entries.shape
    spot = [jax.random.randint(jax.random.fold_in(rng, axis), (), 0, dims[axis]) for axis in range(len(dims))]
    entries = entries.at[tuple(spot)].set(low)
    longest = dims.index(max(dims))
    spot[longest] = (spot[longest] + 1) % dims[longest]
    return entries.at[tuple(spot)].set(high)


def block_levels(own_key, extent, pieces, smallest, high):
    factor_of, own = 1.0, jax.random.fold_in(own_key, 6)
    for dim, blocks in pieces:
        heights = jnp.exp(jax.random.uniform(jax.random.fold_in(own, dim), (blocks,), jnp.float32, smallest / len(pieces), high / len(pieces)))
        factor_of = factor_of * jnp.repeat(heights, extent[dim] // blocks).reshape([-1 if axis == dim else 1 for axis in range(len(extent))])
    return factor_of


def noise(rng, shape, scale, bound, cuts=(), kind=jnp.bfloat16):
    entries = jax.random.normal(rng, shape, jnp.float32) * scale
    if len(cuts) > 0:
        entries = block_levels(rng, shape, cuts, -0.22, 0.18) * entries
    return jnp.clip(entries, min=-bound, max=bound).astype(kind)


def setup_inputs(seed: int = 0) -> dict:
    keys = jax.random.split(jax.random.key(seed), 14)
    layer_input = noise(keys[0], (TOKEN_TOTAL, MODEL_WIDTH), 1.0, 6.0, ((0, 8), (1, 4)))
    value_grad = noise(keys[1], (TOKEN_TOTAL, KV), 1.0, 6.0, ((0, 8), (1, 4)))
    quant_codes = place_ends(jax.random.randint(keys[2], (MODEL_WIDTH, KV), 0, 16), jax.random.fold_in(keys[2], 1), 0, 15).astype(jnp.int32)
    block_scales = jnp.clip(jnp.exp(math.log(0.08) - 1.3862944 * jax.random.uniform(keys[3], (MODEL_WIDTH, KV // QB), jnp.float32) ** block_levels(keys[3], (MODEL_WIDTH, KV // QB), ((0, 8), (1, 4)), -0.2, 0.2)), 0.02, 0.08)
    tenant_ids = place_ends(jax.random.randint(keys[4], (N_FSDP * SLOTS,), 0, TENANTS), jax.random.fold_in(keys[4], 1), 0, TENANTS - 1).astype(jnp.int32)
    live_counts = draw_live_counts(jax.random.fold_in(keys[13], 71), 0)
    tenant_owner = jax.random.permutation(keys[6], TENANTS).astype(jnp.int32)
    factor_down = noise(keys[7], (TENANTS, ADAPTER_RANK, MODEL_WIDTH), 1.0, 6.0, ((0, 8), (2, 4)), jnp.float32)
    factor_up = noise(keys[8], (TENANTS, ADAPTER_RANK, KV), 1.0, 6.0, ((0, 8), (2, 4)), jnp.float32)
    moment_down = noise(keys[9], (TENANTS, ADAPTER_RANK, MODEL_WIDTH), 1.0, 6.0, ((0, 8), (2, 4)), jnp.float32)
    second_down = jnp.clip(jnp.exp(math.log(5.0) - 4.6051702 * jax.random.uniform(keys[10], (TENANTS, ADAPTER_RANK, MODEL_WIDTH), jnp.float32) ** block_levels(keys[10], (TENANTS, ADAPTER_RANK, MODEL_WIDTH), ((0, 8), (2, 4)), -0.2, 0.2)), 0.05, 5.0)
    moment_up = noise(keys[11], (TENANTS, ADAPTER_RANK, KV), 1.0, 6.0, ((0, 8), (2, 4)), jnp.float32)
    second_up = jnp.clip(jnp.exp(math.log(5.0) - 4.6051702 * jax.random.uniform(keys[12], (TENANTS, ADAPTER_RANK, KV), jnp.float32) ** block_levels(keys[12], (TENANTS, ADAPTER_RANK, KV), ((0, 8), (2, 4)), -0.2, 0.2)), 0.05, 5.0)
    return dict(layer_input=layer_input, value_grad=value_grad, quant_codes=quant_codes, block_scales=block_scales, tenant_ids=tenant_ids, live_counts=live_counts, tenant_owner=tenant_owner, factor_down=factor_down, factor_up=factor_up, moment_down=moment_down, second_down=second_down, moment_up=moment_up, second_up=second_up)


nf4_levels = (-1.0, -0.6962, -0.5251, -0.3949, -0.2844, -0.1848, -0.0911, 0.0, 0.0796, 0.1609, 0.2461, 0.3379, 0.4407, 0.5626, 0.723, 1.0)
adapter_scale = 2.0
beta_one = 0.9
beta_two = 0.999
adam_step = 10.0
learn_rate = 0.05
decay_rate = 0.01
adam_eps = 1e-08

def adam_update(param, grad, moment, second):
    new_moment = beta_one * moment + (1.0 - beta_one) * grad
    new_second = beta_two * second + (1.0 - beta_two) * grad * grad
    corrected = new_moment / (1.0 - beta_one ** adam_step)
    divisor = jnp.sqrt(new_second / (1.0 - beta_two ** adam_step)) + adam_eps
    new_param = param - learn_rate * (corrected / divisor + decay_rate * param)
    return (new_param, new_moment, new_second)

def rounded_lower(values):
    lowered = lax.optimization_barrier(values.astype(jnp.bfloat16))
    return lowered.astype(jnp.float32)

def reference(layer_input, value_grad, quant_codes, block_scales, tenant_ids, live_counts, tenant_owner, factor_down, factor_up, moment_down, second_down, moment_up, second_up):
    table = jnp.array(nf4_levels, jnp.float32)
    weight = (jnp.take(table, quant_codes, axis=0) * jnp.repeat(block_scales, QB, axis=1)).astype(jnp.bfloat16)
    seq_index = jnp.arange(N_FSDP * SLOTS, dtype=jnp.int32)
    live_seq = seq_index % SLOTS < jnp.take(live_counts, seq_index // SLOTS, axis=0)
    live_tok = jnp.repeat(live_seq, SEQ)
    masked = jnp.where(live_tok[:, None], value_grad, jnp.zeros_like(value_grad))
    owner_seq = jnp.take(tenant_owner, tenant_ids, axis=0).astype(jnp.int32)
    down_low = factor_down.astype(jnp.bfloat16)
    up_low = factor_up.astype(jnp.bfloat16)
    inverse_width = 1.0 / math.sqrt(MODEL_WIDTH)
    coefficient = adapter_scale / math.sqrt(ADAPTER_RANK)
    base_weight = jnp.dot(masked, weight.T, preferred_element_type=jnp.float32)
    upper_level = lax.Precision.HIGHEST
    block_inputs = layer_input.reshape(N_FSDP, SLOTS, SEQ, MODEL_WIDTH)
    block_gradients = masked.reshape(N_FSDP, SLOTS, SEQ, KV)
    block_owners = owner_seq.reshape(N_FSDP, SLOTS)
    tenant_iota = jnp.arange(TENANTS, dtype=jnp.int32)

    def block_stride(carry, block):
        accumulated_down, accumulated_up = carry
        block_input, block_grad, block_owner = block
        sequence_down = jnp.take(down_low, block_owner, axis=0).astype(jnp.float32)
        sequence_up = jnp.take(up_low, block_owner, axis=0).astype(jnp.float32)
        widened_input = block_input.astype(jnp.float32)
        widened_gradient = block_grad.astype(jnp.float32)
        adapter_input = jnp.einsum('aol,ail->aoi', widened_input, sequence_down, precision=upper_level) * inverse_width
        adapter_gradient = jnp.einsum('qbt,qxt->qbx', widened_gradient, sequence_up, precision=upper_level) * coefficient
        input_lowrank = rounded_lower(adapter_input)
        gradient_lowrank = rounded_lower(adapter_gradient)
        adapter_input_gradient = jnp.einsum('pym,pme->pye', gradient_lowrank, sequence_down, precision=upper_level) * inverse_width
        part_down = jnp.einsum('nsr,nsd->nrd', gradient_lowrank, widened_input, precision=upper_level) * inverse_width
        part_up = jnp.einsum('nsr,nsc->nrc', input_lowrank, widened_gradient, precision=upper_level) * coefficient
        onehot = (block_owner[:, None] == tenant_iota[None, :]).astype(jnp.float32)
        accumulated_down = accumulated_down + jnp.einsum('nt,nrd->trd', onehot, part_down, precision=upper_level)
        accumulated_up = accumulated_up + jnp.einsum('nt,nrc->trc', onehot, part_up, precision=upper_level)
        return ((accumulated_down, accumulated_up), adapter_input_gradient)
    start_offset = (jnp.zeros((TENANTS, ADAPTER_RANK, MODEL_WIDTH), jnp.float32), jnp.zeros((TENANTS, ADAPTER_RANK, KV), jnp.float32))
    (down_gradient, up_gradient), adapter_parts = lax.scan(block_stride, start_offset, (block_inputs, block_gradients, block_owners))
    layer_input_gradient = (base_weight + adapter_parts.reshape(TOKEN_TOTAL, MODEL_WIDTH)).astype(jnp.bfloat16)
    new_down, new_moment_down, new_second_down = adam_update(factor_down, down_gradient, moment_down, second_down)
    new_up, new_moment_up, new_second_up = adam_update(factor_up, up_gradient, moment_up, second_up)
    return (layer_input_gradient, new_down, new_up, new_moment_down, new_second_down, new_moment_up, new_second_up)
```

```python
import functools
import math

import jax
import jax.numpy as jnp
from jax import lax
from jax.experimental import pallas as pl
from jax.experimental.pallas import tpu as pltpu
from jax.sharding import PartitionSpec as P

MODEL_WIDTH = 8192
ADAPTER_RANK = 16


nf4_levels = (
    -1.0,
    -0.6962,
    -0.5251,
    -0.3949,
    -0.2844,
    -0.1848,
    -0.0911,
    0.0,
    0.0796,
    0.1609,
    0.2461,
    0.3379,
    0.4407,
    0.5626,
    0.723,
    1.0,
)
adapter_scale = 2.0
beta_one = 0.9
beta_two = 0.999
adam_step = 10.0
learn_rate = 0.05
decay_rate = 0.01
adam_eps = 1e-08


def adam_update(param, grad, moment, second):
    new_moment = beta_one * moment + (1.0 - beta_one) * grad
    new_second = beta_two * second + (1.0 - beta_two) * grad * grad
    corrected = new_moment / (1.0 - beta_one**adam_step)
    divisor = jnp.sqrt(new_second / (1.0 - beta_two**adam_step)) + adam_eps
    new_param = param - learn_rate * (corrected / divisor + decay_rate * param)
    return (new_param, new_moment, new_second)


def dequantize(quant_codes, block_scales):
    levels_out = jnp.zeros(quant_codes.shape, jnp.float32)
    for position in range(16):
        levels_out = jnp.where(quant_codes == position, nf4_levels[position], levels_out)
    row_count, col_count = quant_codes.shape
    blocks = block_scales.shape[1]
    scaled = levels_out.reshape(row_count, blocks, col_count // blocks) * block_scales[:, :, None]
    return scaled.reshape(row_count, col_count).astype(jnp.bfloat16)


def right_product(left, right):
    return lax.dot_general(
        left, right, (((1,), (1,)), ((), ())), preferred_element_type=jnp.float32
    )


def left_product(left, right):
    return lax.dot_general(
        left, right, (((0,), (0,)), ((), ())), preferred_element_type=jnp.float32
    )


def add_sources(pieces):
    return (jnp.sum(pieces[0], axis=0, keepdims=True), jnp.sum(pieces[1], axis=0, keepdims=True))


def shards(
    layer_input,
    value_grad,
    quant_codes,
    block_scales,
    tenant_ids,
    live_counts,
    tenant_owner,
    factor_down,
    factor_up,
    moment_down,
    second_down,
    moment_up,
    second_up,
):
    tok_rows, width_part = layer_input.shape
    value_part = value_grad.shape[1]
    slot_count = tenant_ids.shape[0]
    seq_len = tok_rows // slot_count
    tenant_total = tenant_owner.shape[0]
    rank_size = factor_down.shape[1]
    inverse_width = 1.0 / math.sqrt(MODEL_WIDTH)
    coefficient = adapter_scale / math.sqrt(ADAPTER_RANK)
    live_seq = jnp.arange(slot_count, dtype=jnp.int32) < live_counts[0]
    live_tok = jnp.broadcast_to(live_seq[:, None], (slot_count, seq_len)).reshape(tok_rows)
    masked = jnp.where(live_tok[:, None], value_grad, jnp.zeros_like(value_grad))
    tenant_iota = jnp.arange(tenant_total, dtype=jnp.int32)
    matches = tenant_ids[:, None] == tenant_iota[None, :]
    slot_seq = jnp.sum(jnp.where(matches, tenant_owner[None, :], 0), axis=1)
    onehot_seq = (slot_seq[:, None] == tenant_iota[None, :]).astype(jnp.bfloat16)
    weight_local = dequantize(quant_codes, block_scales)
    all_down, all_up = (
        lax.all_gather(factor_down.astype(jnp.bfloat16), "fsdp", axis=0, tiled=True),
        lax.all_gather(factor_up.astype(jnp.bfloat16), "fsdp", axis=0, tiled=True),
    )
    partial_value = right_product(masked, lax.all_gather(weight_local, "fsdp", axis=0, tiled=True))
    base_input_grad = lax.psum_scatter(
        partial_value.astype(jnp.bfloat16), "tensor", scatter_dimension=1, tiled=True
    ).astype(jnp.float32)
    flattened_down = all_down.reshape(tenant_total * rank_size, width_part)
    up_flat = all_up.reshape(tenant_total * rank_size, value_part)
    onehot_tok = jnp.broadcast_to(
        onehot_seq[:, None, :], (slot_count, seq_len, tenant_total)
    ).reshape(tok_rows, tenant_total)
    selector = onehot_tok.astype(jnp.float32)[:, :, None]
    down_scores = right_product(layer_input, flattened_down).reshape(
        tok_rows, tenant_total, rank_size
    )
    up_scores = right_product(masked, up_flat).reshape(tok_rows, tenant_total, rank_size)
    in_part = jnp.sum(down_scores * selector, axis=1) * inverse_width
    grad_part = jnp.sum(up_scores * selector, axis=1) * coefficient
    in_sum, grad_sum = lax.psum((in_part, grad_part), "tensor")
    input_lowrank = in_sum.astype(jnp.bfloat16)
    gradient_lowrank = grad_sum.astype(jnp.bfloat16)
    spread_gradient = (onehot_tok[:, :, None] * gradient_lowrank[:, None, :]).reshape(
        tok_rows, tenant_total * rank_size
    )
    in_spread = (onehot_tok[:, :, None] * input_lowrank[:, None, :]).reshape(
        tok_rows, tenant_total * rank_size
    )
    adapter_input_grad = (
        jnp.dot(spread_gradient, flattened_down, preferred_element_type=jnp.float32) * inverse_width
    )
    down_terms = (left_product(spread_gradient, layer_input) * inverse_width).reshape(
        tenant_total, rank_size, width_part
    )
    up_terms = (left_product(in_spread, masked) * coefficient).reshape(
        tenant_total, rank_size, value_part
    )
    down_gradient, up_gradient = add_sources(
        (
            lax.all_to_all(
                down_terms.astype(jnp.bfloat16), "fsdp", split_axis=0, concat_axis=0, tiled=True
            ).astype(down_terms.dtype),
            lax.all_to_all(
                up_terms.astype(jnp.bfloat16), "fsdp", split_axis=0, concat_axis=0, tiled=True
            ).astype(up_terms.dtype),
        )
    )
    layer_input_gradient = (base_input_grad + adapter_input_grad).astype(jnp.bfloat16)
    new_down, new_moment_down, new_second_down = adam_update(
        factor_down, down_gradient, moment_down, second_down
    )
    new_up, new_moment_up, new_second_up = adam_update(factor_up, up_gradient, moment_up, second_up)
    return (
        layer_input_gradient,
        new_down,
        new_up,
        new_moment_down,
        new_second_down,
        new_moment_up,
        new_second_up,
    )


CHUNKS = 4


def level_tree(codes):
    rows = [jnp.float32(level) for level in nf4_levels]
    for bit in range(4):
        chosen = (codes & (1 << bit)) != 0
        rows = [jnp.where(chosen, rows[2 * n + 1], rows[2 * n]) for n in range(len(rows) // 2)]
    return rows[0]


def fused_kernel(
    fsdp,
    tensor,
    ids_ref,
    live_ref,
    owner_ref,
    x_ref,
    dv_ref,
    code_ref,
    scale_ref,
    fd_ref,
    fu_ref,
    md_ref,
    sd_ref,
    mu_ref,
    su_ref,
    out_ref,
    nd_ref,
    nu_ref,
    nmd_ref,
    nsd_ref,
    nmu_ref,
    nsu_ref,
    fac,
    gsend,
    grecv,
    dvs,
    part,
    col,
    wgt,
    outs,
    base,
    fac_s,
    fac_r,
    gr_s,
    gr_r,
    dv_s,
    dvf_s,
    dv_r,
    part_s,
    part_r,
    col_s,
    col_r,
    wgt_s,
    wgt_r,
    out_s,
    out_r,
):
    f = lax.axis_index("fsdp")
    t = lax.axis_index("tensor")
    z, y = f // 2, f % 2
    x, c = t // 2, t % 2
    planes, wide = fsdp // 2, tensor // 2
    tok_rows, width = x_ref.shape
    value = dv_ref.shape[1]
    w_rows = code_ref.shape[0]
    step_rows = w_rows // CHUNKS
    rank = fd_ref.shape[1]
    slots = ids_ref.shape[0]
    seq = tok_rows // slots
    flat = fsdp * rank
    inverse_width = 1.0 / math.sqrt(MODEL_WIDTH)
    coefficient = adapter_scale / math.sqrt(ADAPTER_RANK)
    pending = []

    def remote(src, dst, ss, rs, df, dt):
        return pltpu.make_async_remote_copy(
            src_ref=src,
            dst_ref=dst,
            send_sem=ss,
            recv_sem=rs,
            device_id={"fsdp": df, "tensor": dt},
            device_id_type=pl.DeviceIdType.MESH,
        )

    def send(copy, cond=None):
        if cond is None:
            copy.start()
        else:
            pl.when(cond)(copy.start)
        pending.append((copy, cond))

    barrier = pltpu.get_barrier_semaphore()
    chips = [(dx, dy) for dx in range(wide) for dy in range(2)]
    greeted = 0
    for step in range(1, fsdp):
        pl.semaphore_signal(
            barrier,
            inc=1,
            device_id={"fsdp": (f + step) % fsdp, "tensor": t},
            device_id_type=pl.DeviceIdType.MESH,
        )
        greeted += 1
    for dx, dy in chips:
        for dc in range(2):
            if dx == 0 and dc == 0:
                continue
            pl.semaphore_signal(
                barrier,
                inc=1,
                device_id={
                    "fsdp": 2 * z + (y + dy) % 2,
                    "tensor": 2 * ((x + dx) % wide) + (c + dc) % 2,
                },
                device_id_type=pl.DeviceIdType.MESH,
            )
            greeted += 1

    fac[pl.ds(f, 1), :, 0:width] = fd_ref[...].astype(jnp.bfloat16)
    fac[pl.ds(f, 1), :, width : width + value] = fu_ref[...].astype(jnp.bfloat16)
    tok_index = lax.broadcasted_iota(jnp.int32, (tok_rows, value), 0)
    masked = jnp.where(
        tok_index < live_ref[0] * seq, dv_ref[...].astype(jnp.float32), 0.0
    ).astype(jnp.bfloat16)
    dvs[y, t] = masked

    def dequant(chunk):
        rows = pl.ds(chunk * step_rows, step_rows)
        levels = level_tree(code_ref[rows, :])
        scales = scale_ref[rows, :]
        blocks = scales.shape[1]
        block = value // blocks
        lane = lax.broadcasted_iota(jnp.int32, (step_rows, value), 1)
        spread = jnp.broadcast_to(scales[:, blocks - 1 : blocks], (step_rows, value))
        for n in reversed(range(blocks - 1)):
            spread = jnp.where(lane < (n + 1) * block, scales[:, n : n + 1], spread)
        col[z, rows, :] = (levels * spread).astype(jnp.bfloat16)

    dequant(0)
    pl.semaphore_wait(barrier, greeted)

    def fac_copy(df, source):
        return remote(fac.at[source], fac.at[source], fac_s.at[df], fac_r.at[source], df, t)

    for step in range(1, fsdp):
        send(fac_copy((f + step) % fsdp, f))

    def dv_copy(index, dx, dy, sy, st):
        return remote(
            dvs.at[sy, st],
            dvs.at[sy, st],
            dv_s.at[index],
            dv_r.at[sy, st],
            2 * z + (y + dy) % 2,
            2 * ((x + dx) % wide) + c,
        )

    def dv_forward(index, sy, st):
        return remote(
            dvs.at[sy, st], dvs.at[sy, st], dvf_s.at[index], dv_r.at[sy, st], f, 2 * x + 1 - c
        )

    send(dv_forward(0, y, t))
    for index, (dx, dy) in enumerate(chips):
        if index > 0:
            send(dv_copy(index, dx, dy, y, t))

    def col_copy(way, p, chunk):
        rows = pl.ds(chunk * step_rows, step_rows)
        return remote(
            col.at[p, rows, :],
            col.at[p, rows, :],
            col_s.at[way, p, chunk],
            col_r.at[p, chunk],
            f + (2 if way == 0 else -2),
            t,
        )

    def in_plane(p, chunk, valid):
        rows = pl.ds(chunk * step_rows, step_rows)
        df, dt = 2 * z + p % 2, 2 * (p // 2) + y
        stays = jnp.logical_and(df == f, dt == t)

        @pl.when(jnp.logical_and(valid, stays))
        def _():
            wgt[t, rows, :] = col[p, rows, :]

        copy = remote(
            col.at[p, rows, :],
            wgt.at[t, rows, :],
            wgt_s.at[p, chunk],
            wgt_r.at[t, chunk],
            df,
            dt,
        )
        send(copy, jnp.logical_and(valid, jnp.logical_not(stays)))

    def relay(step):
        for s in range(planes):
            chunk = step - s
            if chunk < 0 or chunk >= CHUNKS:
                continue
            if s == 0:
                send(col_copy(0, z, chunk), z < planes - 1)
                send(col_copy(1, z, chunk), z > 0)
                in_plane(z, chunk, z >= 0)
                continue
            for way in range(2):
                p = z - s if way == 0 else z + s
                valid = p >= 0 if way == 0 else p < planes
                further = z < planes - 1 if way == 0 else z > 0
                held = jnp.clip(p, 0, planes - 1)
                pl.when(valid)(col_copy(way, held, chunk).wait_recv)
                send(col_copy(way, held, chunk), jnp.logical_and(valid, further))
                in_plane(held, chunk, valid)

    relay(0)
    dequant(1)
    relay(1)

    for index, (dx, dy) in enumerate(chips):
        if index > 0:
            sy, st = (y + dy) % 2, 2 * ((x + dx) % wide) + c
            dv_copy(index, dx, dy, sy, st).wait_recv()
            send(dv_forward(index, sy, st))

    slot_row = jnp.zeros((1, tok_rows), jnp.int32)
    seq_row = lax.broadcasted_iota(jnp.int32, (1, tok_rows), 1) // seq
    for n in range(slots):
        own = jnp.int32(0)
        for u in range(fsdp):
            own = own + jnp.where(ids_ref[n] == u, owner_ref[u], 0)
        slot_row = jnp.where(seq_row == n, own, slot_row)
    named = lax.broadcasted_iota(jnp.int32, (flat, tok_rows), 0) // rank
    chosen = named == jnp.broadcast_to(slot_row, (flat, tok_rows))

    for step in range(1, fsdp):
        source = (f + step) % fsdp
        fac_copy(source, source).wait_recv()
    all_down = fac[:, :, 0:width].reshape(flat, width)
    all_up = fac[:, :, width : width + value].reshape(flat, value)

    def folded(scores, factor):
        kept = jnp.where(chosen, scores, 0.0).reshape(fsdp, rank, tok_rows)
        return jnp.sum(kept, axis=0) * factor

    part[t, 0:rank, :] = folded(right_product(all_down, x_ref[...]), inverse_width)
    part[t, rank : 2 * rank, :] = folded(right_product(all_up, masked), coefficient)

    def part_copy(dt, source):
        return remote(part.at[source], part.at[source], part_s.at[dt], part_r.at[source], f, dt)

    for step in range(1, tensor):
        send(part_copy((t + step) % tensor, t))

    dequant(2)
    relay(2)
    dequant(3)

    for step in range(1, tensor):
        source = (t + step) % tensor
        part_copy(source, source).wait_recv()
    sums = jnp.sum(part[...], axis=0)
    low = sums.astype(jnp.bfloat16).astype(jnp.float32)

    def spread_out(rows):
        tiled = jnp.broadcast_to(rows[None], (fsdp, rank, tok_rows)).reshape(flat, tok_rows)
        return jnp.where(chosen, tiled, 0.0).astype(jnp.bfloat16)

    in_spread = spread_out(low[0:rank])
    grad_spread = spread_out(low[rank : 2 * rank])
    down_terms = jnp.dot(grad_spread, x_ref[...], preferred_element_type=jnp.float32)
    gsend[:, :, 0:width] = (
        (down_terms * inverse_width).astype(jnp.bfloat16).reshape(fsdp, rank, width)
    )
    up_terms = jnp.dot(in_spread, masked, preferred_element_type=jnp.float32)
    gsend[:, :, width : width + value] = (
        (up_terms * coefficient).astype(jnp.bfloat16).reshape(fsdp, rank, value)
    )

    def grad_copy(df, source):
        return remote(gsend.at[df], grecv.at[source], gr_s.at[df], gr_r.at[source], df, t)

    for step in range(1, fsdp):
        send(grad_copy((f + step) % fsdp, f))
    grecv[pl.ds(f, 1)] = gsend[pl.ds(f, 1)]

    relay(3)

    for sy in range(2):
        for st in range(tensor):
            pl.when(st % 2 != c)(dv_forward(0, sy, st).wait_recv)

    def multiply(chunk):
        rows = pl.ds(chunk * step_rows, step_rows)
        for st in range(tensor):
            stays = jnp.logical_and(c == y, t == st)
            arrived = remote(
                col.at[0, rows, :],
                wgt.at[st, rows, :],
                wgt_s.at[0, chunk],
                wgt_r.at[st, chunk],
                f,
                t,
            )
            pl.when(jnp.logical_not(stays))(arrived.wait_recv)
        for half in range(2):
            total = right_product(dvs[half, 0], wgt[0, rows, :])
            for st in range(1, tensor):
                total = total + right_product(dvs[half, st], wgt[st, rows, :])
            outs[half, chunk] = total.astype(jnp.bfloat16)
            df, dt = 2 * z + half, 2 * x + y
            stays = jnp.logical_and(df == f, dt == t)

            @pl.when(stays)
            def _():
                base[c, chunk] = outs[half, chunk]

            copy = remote(
                outs.at[half, chunk],
                base.at[c, chunk],
                out_s.at[half, chunk],
                out_r.at[c, chunk],
                df,
                dt,
            )
            send(copy, jnp.logical_not(stays))

    for step in range(planes, CHUNKS + planes - 1):
        relay(step)
        multiply(step - planes)

    for step in range(1, fsdp):
        source = (f + step) % fsdp
        grad_copy(source, source).wait_recv()
    multiply(CHUNKS - 1)

    down_grad = jnp.sum(grecv[:, :, 0:width].astype(jnp.float32), axis=0, keepdims=True)
    up_grad = jnp.sum(
        grecv[:, :, width : width + value].astype(jnp.float32), axis=0, keepdims=True
    )
    nd_ref[...], nmd_ref[...], nsd_ref[...] = adam_update(
        fd_ref[...], down_grad, md_ref[...], sd_ref[...]
    )
    nu_ref[...], nmu_ref[...], nsu_ref[...] = adam_update(
        fu_ref[...], up_grad, mu_ref[...], su_ref[...]
    )

    for chunk in range(CHUNKS):
        for half in range(2):
            stays = jnp.logical_and(half == c, c == f % 2)
            arrived = remote(
                outs.at[0, chunk],
                base.at[half, chunk],
                out_s.at[0, chunk],
                out_r.at[half, chunk],
                f,
                t,
            )
            pl.when(jnp.logical_not(stays))(arrived.wait_recv)
            start = half * w_rows + chunk * step_rows
            low_term = lax.dot_general(
                grad_spread,
                fac[:, :, start : start + step_rows].reshape(flat, step_rows),
                (((0,), (0,)), ((), ())),
                preferred_element_type=jnp.float32,
            )
            out_ref[:, start : start + step_rows] = (
                base[half, chunk].astype(jnp.float32) + low_term * inverse_width
            ).astype(jnp.bfloat16)

    for copy, cond in pending:
        if cond is None:
            copy.wait_send()
        else:
            pl.when(cond)(copy.wait_send)


def fused(fsdp, tensor, *args):
    (
        layer_input,
        value_grad,
        quant_codes,
        block_scales,
        tenant_ids,
        live_counts,
        tenant_owner,
        factor_down,
        factor_up,
        moment_down,
        second_down,
        moment_up,
        second_up,
    ) = args
    tok_rows, width = layer_input.shape
    value = value_grad.shape[1]
    w_rows = quant_codes.shape[0]
    rank = factor_down.shape[1]
    step_rows = w_rows // CHUNKS
    low = jnp.bfloat16
    dma = pltpu.SemaphoreType.DMA
    smem = pl.BlockSpec(memory_space=pltpu.SMEM)
    vmem = pl.BlockSpec(memory_space=pltpu.VMEM)
    like = jax.ShapeDtypeStruct
    return pl.pallas_call(
        functools.partial(fused_kernel, fsdp, tensor),
        out_shape=(
            like(layer_input.shape, low),
            like(factor_down.shape, jnp.float32),
            like(factor_up.shape, jnp.float32),
            like(factor_down.shape, jnp.float32),
            like(factor_down.shape, jnp.float32),
            like(factor_up.shape, jnp.float32),
            like(factor_up.shape, jnp.float32),
        ),
        in_specs=[smem] * 3 + [vmem] * 10,
        out_specs=(vmem,) * 7,
        scratch_shapes=[
            pltpu.VMEM((fsdp, rank, width + value), low),
            pltpu.VMEM((fsdp, rank, width + value), low),
            pltpu.VMEM((fsdp, rank, width + value), low),
            pltpu.VMEM((2, tensor, tok_rows, value), low),
            pltpu.VMEM((tensor, 2 * rank, tok_rows), jnp.float32),
            pltpu.VMEM((fsdp // 2, w_rows, value), low),
            pltpu.VMEM((tensor, w_rows, value), low),
            pltpu.VMEM((2, CHUNKS, tok_rows, step_rows), low),
            pltpu.VMEM((2, CHUNKS, tok_rows, step_rows), low),
            dma((fsdp,)),
            dma((fsdp,)),
            dma((fsdp,)),
            dma((fsdp,)),
            dma((tensor,)),
            dma((tensor,)),
            dma((2, tensor)),
            dma((tensor,)),
            dma((tensor,)),
            dma((2, fsdp // 2, CHUNKS)),
            dma((fsdp // 2, CHUNKS)),
            dma((fsdp // 2, CHUNKS)),
            dma((tensor, CHUNKS)),
            dma((2, CHUNKS)),
            dma((2, CHUNKS)),
        ],
        compiler_params=pltpu.CompilerParams(
            collective_id=0, has_side_effects=True, vmem_limit_bytes=40 * 1024 * 1024
        ),
    )(
        tenant_ids,
        live_counts,
        tenant_owner,
        layer_input,
        value_grad,
        quant_codes,
        block_scales,
        factor_down,
        factor_up,
        moment_down,
        second_down,
        moment_up,
        second_up,
    )


def solution(mesh):
    fsdp, tensor = mesh.shape["fsdp"], mesh.shape["tensor"]
    planar = fsdp == 2 * tensor and tensor % 2 == 0
    body = functools.partial(fused, fsdp, tensor) if planar else shards
    in_specs = (
        P("fsdp", "tensor"),
        P("fsdp", "tensor"),
        P("fsdp", "tensor"),
        P("fsdp", "tensor"),
        P("fsdp"),
        P("fsdp"),
        P(),
        P("fsdp", None, "tensor"),
        P("fsdp", None, "tensor"),
        P("fsdp", None, "tensor"),
        P("fsdp", None, "tensor"),
        P("fsdp", None, "tensor"),
        P("fsdp", None, "tensor"),
    )
    out_specs = (
        P("fsdp", "tensor"),
        P("fsdp", None, "tensor"),
        P("fsdp", None, "tensor"),
        P("fsdp", None, "tensor"),
        P("fsdp", None, "tensor"),
        P("fsdp", None, "tensor"),
        P("fsdp", None, "tensor"),
    )
    return jax.shard_map(body, mesh=mesh, in_specs=in_specs, out_specs=out_specs, check_vma=False)
```

```python
import functools
import math

import jax
import jax.numpy as jnp
from jax import lax
from jax.experimental import pallas as pl
from jax.experimental.pallas import tpu as pltpu
from jax.sharding import PartitionSpec as P

MODEL_WIDTH = 8192
ADAPTER_RANK = 16


nf4_levels = (
    -1.0,
    -0.6962,
    -0.5251,
    -0.3949,
    -0.2844,
    -0.1848,
    -0.0911,
    0.0,
    0.0796,
    0.1609,
    0.2461,
    0.3379,
    0.4407,
    0.5626,
    0.723,
    1.0,
)
adapter_scale = 2.0
beta_one = 0.9
beta_two = 0.999
adam_step = 10.0
learn_rate = 0.05
decay_rate = 0.01
adam_eps = 1e-08


def adam_update(param, grad, moment, second):
    new_moment = beta_one * moment + (1.0 - beta_one) * grad
    new_second = beta_two * second + (1.0 - beta_two) * grad * grad
    corrected = new_moment / (1.0 - beta_one**adam_step)
    divisor = jnp.sqrt(new_second / (1.0 - beta_two**adam_step)) + adam_eps
    new_param = param - learn_rate * (corrected / divisor + decay_rate * param)
    return (new_param, new_moment, new_second)


def dequantize(quant_codes, block_scales):
    levels_out = jnp.zeros(quant_codes.shape, jnp.float32)
    for position in range(16):
        levels_out = jnp.where(quant_codes == position, nf4_levels[position], levels_out)
    row_count, col_count = quant_codes.shape
    blocks = block_scales.shape[1]
    scaled = levels_out.reshape(row_count, blocks, col_count // blocks) * block_scales[:, :, None]
    return scaled.reshape(row_count, col_count).astype(jnp.bfloat16)


def right_product(left, right):
    return lax.dot_general(
        left, right, (((1,), (1,)), ((), ())), preferred_element_type=jnp.float32
    )


def left_product(left, right):
    return lax.dot_general(
        left, right, (((0,), (0,)), ((), ())), preferred_element_type=jnp.float32
    )


def add_sources(pieces):
    return (jnp.sum(pieces[0], axis=0, keepdims=True), jnp.sum(pieces[1], axis=0, keepdims=True))


def shards(
    layer_input,
    value_grad,
    quant_codes,
    block_scales,
    tenant_ids,
    live_counts,
    tenant_owner,
    factor_down,
    factor_up,
    moment_down,
    second_down,
    moment_up,
    second_up,
):
    tok_rows, width_part = layer_input.shape
    value_part = value_grad.shape[1]
    slot_count = tenant_ids.shape[0]
    seq_len = tok_rows // slot_count
    tenant_total = tenant_owner.shape[0]
    rank_size = factor_down.shape[1]
    inverse_width = 1.0 / math.sqrt(MODEL_WIDTH)
    coefficient = adapter_scale / math.sqrt(ADAPTER_RANK)
    live_seq = jnp.arange(slot_count, dtype=jnp.int32) < live_counts[0]
    live_tok = jnp.broadcast_to(live_seq[:, None], (slot_count, seq_len)).reshape(tok_rows)
    masked = jnp.where(live_tok[:, None], value_grad, jnp.zeros_like(value_grad))
    tenant_iota = jnp.arange(tenant_total, dtype=jnp.int32)
    matches = tenant_ids[:, None] == tenant_iota[None, :]
    slot_seq = jnp.sum(jnp.where(matches, tenant_owner[None, :], 0), axis=1)
    onehot_seq = (slot_seq[:, None] == tenant_iota[None, :]).astype(jnp.bfloat16)
    weight_local = dequantize(quant_codes, block_scales)
    all_down, all_up = (
        lax.all_gather(factor_down.astype(jnp.bfloat16), "fsdp", axis=0, tiled=True),
        lax.all_gather(factor_up.astype(jnp.bfloat16), "fsdp", axis=0, tiled=True),
    )
    partial_value = right_product(masked, lax.all_gather(weight_local, "fsdp", axis=0, tiled=True))
    base_input_grad = lax.psum_scatter(
        partial_value.astype(jnp.bfloat16), "tensor", scatter_dimension=1, tiled=True
    ).astype(jnp.float32)
    flattened_down = all_down.reshape(tenant_total * rank_size, width_part)
    up_flat = all_up.reshape(tenant_total * rank_size, value_part)
    onehot_tok = jnp.broadcast_to(
        onehot_seq[:, None, :], (slot_count, seq_len, tenant_total)
    ).reshape(tok_rows, tenant_total)
    selector = onehot_tok.astype(jnp.float32)[:, :, None]
    down_scores = right_product(layer_input, flattened_down).reshape(
        tok_rows, tenant_total, rank_size
    )
    up_scores = right_product(masked, up_flat).reshape(tok_rows, tenant_total, rank_size)
    in_part = jnp.sum(down_scores * selector, axis=1) * inverse_width
    grad_part = jnp.sum(up_scores * selector, axis=1) * coefficient
    in_sum, grad_sum = lax.psum((in_part, grad_part), "tensor")
    input_lowrank = in_sum.astype(jnp.bfloat16)
    gradient_lowrank = grad_sum.astype(jnp.bfloat16)
    spread_gradient = (onehot_tok[:, :, None] * gradient_lowrank[:, None, :]).reshape(
        tok_rows, tenant_total * rank_size
    )
    in_spread = (onehot_tok[:, :, None] * input_lowrank[:, None, :]).reshape(
        tok_rows, tenant_total * rank_size
    )
    adapter_input_grad = (
        jnp.dot(spread_gradient, flattened_down, preferred_element_type=jnp.float32) * inverse_width
    )
    down_terms = (left_product(spread_gradient, layer_input) * inverse_width).reshape(
        tenant_total, rank_size, width_part
    )
    up_terms = (left_product(in_spread, masked) * coefficient).reshape(
        tenant_total, rank_size, value_part
    )
    down_gradient, up_gradient = add_sources(
        (
            lax.all_to_all(
                down_terms.astype(jnp.bfloat16), "fsdp", split_axis=0, concat_axis=0, tiled=True
            ).astype(down_terms.dtype),
            lax.all_to_all(
                up_terms.astype(jnp.bfloat16), "fsdp", split_axis=0, concat_axis=0, tiled=True
            ).astype(up_terms.dtype),
        )
    )
    layer_input_gradient = (base_input_grad + adapter_input_grad).astype(jnp.bfloat16)
    new_down, new_moment_down, new_second_down = adam_update(
        factor_down, down_gradient, moment_down, second_down
    )
    new_up, new_moment_up, new_second_up = adam_update(factor_up, up_gradient, moment_up, second_up)
    return (
        layer_input_gradient,
        new_down,
        new_up,
        new_moment_down,
        new_second_down,
        new_moment_up,
        new_second_up,
    )


CHUNKS = 4


def level_tree(codes):
    rows = [jnp.float32(level) for level in nf4_levels]
    for bit in range(4):
        chosen = (codes & (1 << bit)) != 0
        rows = [jnp.where(chosen, rows[2 * n + 1], rows[2 * n]) for n in range(len(rows) // 2)]
    return rows[0]


def fused_kernel(
    fsdp,
    tensor,
    ids_any,
    live_any,
    owner_any,
    x_any,
    dv_any,
    code_any,
    scale_any,
    fd_any,
    fu_any,
    out_ref,
    dg_ref,
    ug_ref,
    ids_ref,
    live_ref,
    owner_ref,
    x_ref,
    dv_ref,
    code_ref,
    scale_ref,
    fd_ref,
    fu_ref,
    in_s,
    fac,
    gsend,
    gy,
    gz,
    grecv,
    dvs,
    part,
    col,
    wgt,
    outs,
    base,
    fac_s,
    fac_f,
    fac_r,
    gy_s,
    gy_r,
    gz_s,
    gz_r,
    dv_s,
    dvf_s,
    dv_r,
    part_s,
    part_r,
    col_s,
    col_r,
    wgt_s,
    wgt_r,
    out_s,
    out_r,
):
    f = lax.axis_index("fsdp")
    t = lax.axis_index("tensor")
    z, y = f // 2, f % 2
    x, c = t // 2, t % 2
    planes, wide = fsdp // 2, tensor // 2
    tok_rows, width = x_ref.shape
    value = dv_ref.shape[1]
    w_rows = code_ref.shape[0]
    step_rows = w_rows // CHUNKS
    rank = fd_ref.shape[1]
    slots = ids_ref.shape[0]
    seq = tok_rows // slots
    flat = fsdp * rank
    inverse_width = 1.0 / math.sqrt(MODEL_WIDTH)
    coefficient = adapter_scale / math.sqrt(ADAPTER_RANK)
    pending = []

    loads = {}
    for n, (name, src, dst) in enumerate(
        (
            ("fd", fd_any, fd_ref),
            ("fu", fu_any, fu_ref),
            ("dv", dv_any, dv_ref),
            ("live", live_any, live_ref),
            ("scale", scale_any, scale_ref),
            ("code", code_any, code_ref),
            ("x", x_any, x_ref),
            ("ids", ids_any, ids_ref),
            ("owner", owner_any, owner_ref),
        )
    ):
        loads[name] = pltpu.make_async_copy(src, dst, in_s.at[n])
        loads[name].start()

    def remote(src, dst, ss, rs, df, dt):
        return pltpu.make_async_remote_copy(
            src_ref=src,
            dst_ref=dst,
            send_sem=ss,
            recv_sem=rs,
            device_id={"fsdp": df, "tensor": dt},
            device_id_type=pl.DeviceIdType.MESH,
        )

    def send(copy, cond=None):
        if cond is None:
            copy.start()
        else:
            pl.when(cond)(copy.start)
        pending.append((copy, cond))

    barrier = pltpu.get_barrier_semaphore()
    chips = [(dx, dy) for dx in range(wide) for dy in range(2)]
    greeted = 0
    for step in range(1, fsdp):
        pl.semaphore_signal(
            barrier,
            inc=1,
            device_id={"fsdp": (f + step) % fsdp, "tensor": t},
            device_id_type=pl.DeviceIdType.MESH,
        )
        greeted += 1
    for dx, dy in chips:
        for dc in range(2):
            if dx == 0 and dc == 0:
                continue
            pl.semaphore_signal(
                barrier,
                inc=1,
                device_id={
                    "fsdp": 2 * z + (y + dy) % 2,
                    "tensor": 2 * ((x + dx) % wide) + (c + dc) % 2,
                },
                device_id_type=pl.DeviceIdType.MESH,
            )
            greeted += 1

    loads["fd"].wait()
    loads["fu"].wait()
    fac[pl.ds(f, 1), :, 0:width] = fd_ref[...].astype(jnp.bfloat16)
    fac[pl.ds(f, 1), :, width : width + value] = fu_ref[...].astype(jnp.bfloat16)
    loads["dv"].wait()
    loads["live"].wait()
    tok_index = lax.broadcasted_iota(jnp.int32, (tok_rows, value), 0)
    masked = jnp.where(
        tok_index < live_ref[0] * seq, dv_ref[...].astype(jnp.float32), 0.0
    ).astype(jnp.bfloat16)
    dvs[t, y] = masked

    def dequant(chunk):
        rows = pl.ds(chunk * step_rows, step_rows)
        levels = level_tree(code_ref[rows, :])
        scales = jnp.transpose(scale_ref[:, rows])
        blocks = scales.shape[1]
        block = value // blocks
        lane = lax.broadcasted_iota(jnp.int32, (step_rows, value), 1)
        spread = jnp.broadcast_to(scales[:, blocks - 1 : blocks], (step_rows, value))
        for n in reversed(range(blocks - 1)):
            spread = jnp.where(lane < (n + 1) * block, scales[:, n : n + 1], spread)
        col[z, rows, :] = (levels * spread).astype(jnp.bfloat16)

    pl.semaphore_wait(barrier, greeted)

    def fac_copy(dz, source):
        return remote(
            fac.at[source], fac.at[source], fac_s.at[dz], fac_r.at[source], (f + 2 * dz) % fsdp, t
        )

    def fac_forward(dz, source):
        return remote(
            fac.at[source], fac.at[source], fac_f.at[dz], fac_r.at[source], 2 * z + 1 - y, t
        )

    for dz in range(1, planes):
        send(fac_copy(dz, f))
    send(fac_forward(0, f))

    across = remote(
        dvs.at[t, y], dvs.at[t, y], dv_s.at[0], dv_r.at[t, y], 2 * z + 1 - y, t
    )
    across_in = remote(
        dvs.at[t, 1 - y], dvs.at[t, 1 - y], dv_s.at[0], dv_r.at[t, 1 - y], 2 * z + 1 - y, t
    )
    send(across)

    def dv_copy(dx, st):
        return remote(
            dvs.at[st],
            dvs.at[st],
            dv_s.at[dx],
            dv_r.at[st, 0],
            f,
            2 * ((x + dx) % wide) + c,
        )

    def dv_forward(dx, st):
        return remote(dvs.at[st], dvs.at[st], dvf_s.at[dx], dv_r.at[st, 0], f, 2 * x + 1 - c)

    def col_copy(way, p, chunk):
        rows = pl.ds(chunk * step_rows, step_rows)
        return remote(
            col.at[p, rows, :],
            col.at[p, rows, :],
            col_s.at[way, p, chunk],
            col_r.at[p, chunk],
            f + (2 if way == 0 else -2),
            t,
        )

    def in_plane(p, chunk, valid):
        rows = pl.ds(chunk * step_rows, step_rows)
        df, dt = 2 * z + p % 2, 2 * (p // 2) + y
        stays = jnp.logical_and(df == f, dt == t)

        @pl.when(jnp.logical_and(valid, stays))
        def _():
            wgt[t, rows, :] = col[p, rows, :]

        copy = remote(
            col.at[p, rows, :],
            wgt.at[t, rows, :],
            wgt_s.at[p, chunk],
            wgt_r.at[t, chunk],
            df,
            dt,
        )
        send(copy, jnp.logical_and(valid, jnp.logical_not(stays)))

    def own(chunk):
        send(col_copy(0, z, chunk), z < planes - 1)
        send(col_copy(1, z, chunk), z > 0)
        in_plane(z, chunk, z >= 0)

    def relay(step):
        for s in range(1, planes):
            chunk = step - s
            if chunk < 0 or chunk >= CHUNKS:
                continue
            for way in range(2):
                p = z - s if way == 0 else z + s
                valid = p >= 0 if way == 0 else p < planes
                further = z < planes - 1 if way == 0 else z > 0
                held = jnp.clip(p, 0, planes - 1)
                pl.when(valid)(col_copy(way, held, chunk).wait_recv)
                send(col_copy(way, held, chunk), jnp.logical_and(valid, further))
                in_plane(held, chunk, valid)

    loads["scale"].wait()
    loads["code"].wait()
    for chunk in range(CHUNKS):
        dequant(chunk)
        own(chunk)

    for dz in range(1, planes):
        source = (f + 2 * dz) % fsdp
        fac_copy(dz, source).wait_recv()
        send(fac_forward(dz, source))
    across_in.wait_recv()
    for dx in range(1, wide):
        send(dv_copy(dx, t))
    send(dv_forward(0, t))
    relay(1)

    loads["ids"].wait()
    loads["owner"].wait()
    slot_row = jnp.zeros((1, tok_rows), jnp.int32)
    seq_row = lax.broadcasted_iota(jnp.int32, (1, tok_rows), 1) // seq
    for n in range(slots):
        own = jnp.int32(0)
        for u in range(fsdp):
            own = own + jnp.where(ids_ref[n] == u, owner_ref[u], 0)
        slot_row = jnp.where(seq_row == n, own, slot_row)
    named = lax.broadcasted_iota(jnp.int32, (flat, tok_rows), 0) // rank
    chosen = named == jnp.broadcast_to(slot_row, (flat, tok_rows))

    relay(2)
    for dz in range(planes):
        source = (2 * z + 2 * dz) % fsdp + 1 - y
        fac_forward(dz, source).wait_recv()
    loads["x"].wait()
    all_down = fac[:, :, 0:width].reshape(flat, width)
    all_up = fac[:, :, width : width + value].reshape(flat, value)

    def folded(scores, factor):
        kept = jnp.where(chosen, scores, 0.0).reshape(fsdp, rank, tok_rows)
        return jnp.sum(kept, axis=0) * factor

    part[t, 0:rank, :] = folded(right_product(all_down, x_ref[...]), inverse_width)
    part[t, rank : 2 * rank, :] = folded(right_product(all_up, masked), coefficient)

    def part_copy(dt, source):
        return remote(part.at[source], part.at[source], part_s.at[dt], part_r.at[source], f, dt)

    for step in range(1, tensor):
        send(part_copy((t + step) % tensor, t))

    relay(3)
    for dx in range(1, wide):
        st = 2 * ((x + dx) % wide) + c
        dv_copy(dx, st).wait_recv()
        send(dv_forward(dx, st))

    for step in range(1, tensor):
        source = (t + step) % tensor
        part_copy(source, source).wait_recv()
    sums = jnp.sum(part[...], axis=0)
    low = sums.astype(jnp.bfloat16).astype(jnp.float32)

    def spread_out(rows):
        tiled = jnp.broadcast_to(rows[None], (fsdp, rank, tok_rows)).reshape(flat, tok_rows)
        return jnp.where(chosen, tiled, 0.0).astype(jnp.bfloat16)

    in_spread = spread_out(low[0:rank])
    grad_spread = spread_out(low[rank : 2 * rank])
    down_terms = jnp.dot(grad_spread, x_ref[...], preferred_element_type=jnp.float32)
    by_slot = (down_terms * inverse_width).astype(jnp.bfloat16).reshape(fsdp, rank, width)
    up_terms = jnp.dot(in_spread, masked, preferred_element_type=jnp.float32)
    up_slot = (up_terms * coefficient).astype(jnp.bfloat16).reshape(fsdp, rank, value)
    for slot in range(fsdp):
        gsend[slot % 2, slot // 2, :, 0:width] = by_slot[slot]
        gsend[slot % 2, slot // 2, :, width : width + value] = up_slot[slot]
    over = remote(gsend.at[1 - y], gy, gy_s.at[0], gy_r.at[0], 2 * z + 1 - y, t)
    send(over)

    def grad_copy(dz, to, source):
        return remote(
            gz.at[to], grecv.at[source], gz_s.at[dz], gz_r.at[source], (f + 2 * dz) % fsdp, t
        )

    relay(4)
    for st in range(tensor):
        pl.when(st % 2 != c)(dv_forward(0, st).wait_recv)

    def multiply(chunk):
        rows = pl.ds(chunk * step_rows, step_rows)
        for st in range(tensor):
            stays = jnp.logical_and(c == y, t == st)
            arrived = remote(
                col.at[0, rows, :],
                wgt.at[st, rows, :],
                wgt_s.at[0, chunk],
                wgt_r.at[st, chunk],
                f,
                t,
            )
            pl.when(jnp.logical_not(stays))(arrived.wait_recv)
        for half in range(2):
            total = right_product(dvs[0, half], wgt[0, rows, :])
            for st in range(1, tensor):
                total = total + right_product(dvs[st, half], wgt[st, rows, :])
            outs[half, chunk] = total.astype(jnp.bfloat16)
            df, dt = 2 * z + half, 2 * x + y
            stays = jnp.logical_and(df == f, dt == t)

            @pl.when(stays)
            def _():
                base[c, chunk] = outs[half, chunk]

            copy = remote(
                outs.at[half, chunk],
                base.at[c, chunk],
                out_s.at[half, chunk],
                out_r.at[c, chunk],
                df,
                dt,
            )
            send(copy, jnp.logical_not(stays))

    multiply(0)
    over.wait_recv()
    gz[...] = (gsend[y].astype(jnp.float32) + gy[...].astype(jnp.float32)).astype(jnp.bfloat16)
    for dz in range(1, planes):
        send(grad_copy(dz, (z + dz) % planes, z))
    grecv[pl.ds(z, 1)] = gz[pl.ds(z, 1)]

    for step in range(5, CHUNKS + planes):
        relay(step)
        if step - planes < CHUNKS - 1:
            multiply(step - planes)
    for dz in range(1, planes):
        grad_copy(dz, 0, (z + dz) % planes).wait_recv()
    dg_ref[...] = jnp.sum(grecv[:, :, 0:width].astype(jnp.float32), axis=0, keepdims=True)
    ug_ref[...] = jnp.sum(
        grecv[:, :, width : width + value].astype(jnp.float32), axis=0, keepdims=True
    )
    multiply(CHUNKS - 1)

    for chunk in range(CHUNKS):
        for half in range(2):
            stays = jnp.logical_and(half == c, c == f % 2)
            arrived = remote(
                outs.at[0, chunk],
                base.at[half, chunk],
                out_s.at[0, chunk],
                out_r.at[half, chunk],
                f,
                t,
            )
            pl.when(jnp.logical_not(stays))(arrived.wait_recv)
            start = half * w_rows + chunk * step_rows
            low_term = lax.dot_general(
                grad_spread,
                fac[:, :, start : start + step_rows].reshape(flat, step_rows),
                (((0,), (0,)), ((), ())),
                preferred_element_type=jnp.float32,
            )
            out_ref[:, start : start + step_rows] = (
                base[half, chunk].astype(jnp.float32) + low_term * inverse_width
            ).astype(jnp.bfloat16)

    for copy, cond in pending:
        if cond is None:
            copy.wait_send()
        else:
            pl.when(cond)(copy.wait_send)


def fused(fsdp, tensor, *args):
    (
        layer_input,
        value_grad,
        quant_codes,
        block_scales,
        tenant_ids,
        live_counts,
        tenant_owner,
        factor_down,
        factor_up,
        moment_down,
        second_down,
        moment_up,
        second_up,
    ) = args
    tok_rows, width = layer_input.shape
    value = value_grad.shape[1]
    w_rows = quant_codes.shape[0]
    rank = factor_down.shape[1]
    step_rows = w_rows // CHUNKS
    low = jnp.bfloat16
    dma = pltpu.SemaphoreType.DMA
    vmem = pl.BlockSpec(memory_space=pltpu.VMEM)
    like = jax.ShapeDtypeStruct
    layer_input_gradient, down_gradient, up_gradient = pl.pallas_call(
        functools.partial(fused_kernel, fsdp, tensor),
        out_shape=(
            like(layer_input.shape, low),
            like(factor_down.shape, jnp.float32),
            like(factor_up.shape, jnp.float32),
        ),
        in_specs=[pl.BlockSpec(memory_space=pl.ANY)] * 9,
        out_specs=(vmem,) * 3,
        scratch_shapes=[
            pltpu.SMEM(tenant_ids.shape, jnp.int32),
            pltpu.SMEM(live_counts.shape, jnp.int32),
            pltpu.SMEM(tenant_owner.shape, jnp.int32),
            pltpu.VMEM(layer_input.shape, low),
            pltpu.VMEM(value_grad.shape, low),
            pltpu.VMEM(quant_codes.shape, jnp.int32),
            pltpu.VMEM(block_scales.shape[::-1], jnp.float32),
            pltpu.VMEM(factor_down.shape, jnp.float32),
            pltpu.VMEM(factor_up.shape, jnp.float32),
            dma((9,)),
            pltpu.VMEM((fsdp, rank, width + value), low),
            pltpu.VMEM((2, fsdp // 2, rank, width + value), low),
            pltpu.VMEM((fsdp // 2, rank, width + value), low),
            pltpu.VMEM((fsdp // 2, rank, width + value), low),
            pltpu.VMEM((fsdp // 2, rank, width + value), low),
            pltpu.VMEM((tensor, 2, tok_rows, value), low),
            pltpu.VMEM((tensor, 2 * rank, tok_rows), jnp.float32),
            pltpu.VMEM((fsdp // 2, w_rows, value), low),
            pltpu.VMEM((tensor, w_rows, value), low),
            pltpu.VMEM((2, CHUNKS, tok_rows, step_rows), low),
            pltpu.VMEM((2, CHUNKS, tok_rows, step_rows), low),
            dma((fsdp // 2,)),
            dma((fsdp // 2,)),
            dma((fsdp,)),
            dma((1,)),
            dma((1,)),
            dma((fsdp // 2,)),
            dma((fsdp // 2,)),
            dma((tensor // 2,)),
            dma((tensor // 2,)),
            dma((tensor, 2)),
            dma((tensor,)),
            dma((tensor,)),
            dma((2, fsdp // 2, CHUNKS)),
            dma((fsdp // 2, CHUNKS)),
            dma((fsdp // 2, CHUNKS)),
            dma((tensor, CHUNKS)),
            dma((2, CHUNKS)),
            dma((2, CHUNKS)),
        ],
        compiler_params=pltpu.CompilerParams(
            collective_id=0, has_side_effects=True, vmem_limit_bytes=56 * 1024 * 1024
        ),
    )(
        tenant_ids,
        live_counts,
        tenant_owner,
        layer_input,
        value_grad,
        quant_codes,
        block_scales.T,
        factor_down,
        factor_up,
    )
    new_down, new_moment_down, new_second_down = adam_update(
        factor_down, down_gradient, moment_down, second_down
    )
    new_up, new_moment_up, new_second_up = adam_update(factor_up, up_gradient, moment_up, second_up)
    return (
        layer_input_gradient,
        new_down,
        new_up,
        new_moment_down,
        new_second_down,
        new_moment_up,
        new_second_up,
    )


def solution(mesh):
    fsdp, tensor = mesh.shape["fsdp"], mesh.shape["tensor"]
    planar = fsdp == 2 * tensor and tensor % 2 == 0
    body = functools.partial(fused, fsdp, tensor) if planar else shards
    in_specs = (
        P("fsdp", "tensor"),
        P("fsdp", "tensor"),
        P("fsdp", "tensor"),
        P("fsdp", "tensor"),
        P("fsdp"),
        P("fsdp"),
        P(),
        P("fsdp", None, "tensor"),
        P("fsdp", None, "tensor"),
        P("fsdp", None, "tensor"),
        P("fsdp", None, "tensor"),
        P("fsdp", None, "tensor"),
        P("fsdp", None, "tensor"),
    )
    out_specs = (
        P("fsdp", "tensor"),
        P("fsdp", None, "tensor"),
        P("fsdp", None, "tensor"),
        P("fsdp", None, "tensor"),
        P("fsdp", None, "tensor"),
        P("fsdp", None, "tensor"),
        P("fsdp", None, "tensor"),
    )
    return jax.shard_map(body, mesh=mesh, in_specs=in_specs, out_specs=out_specs, check_vma=False)
```

```python
import functools
import math

import jax
import jax.numpy as jnp
from jax import lax
from jax.experimental import pallas as pl
from jax.experimental.pallas import tpu as pltpu
from jax.sharding import PartitionSpec as P

MODEL_WIDTH = 8192
ADAPTER_RANK = 16


nf4_levels = (
    -1.0,
    -0.6962,
    -0.5251,
    -0.3949,
    -0.2844,
    -0.1848,
    -0.0911,
    0.0,
    0.0796,
    0.1609,
    0.2461,
    0.3379,
    0.4407,
    0.5626,
    0.723,
    1.0,
)
adapter_scale = 2.0
beta_one = 0.9
beta_two = 0.999
adam_step = 10.0
learn_rate = 0.05
decay_rate = 0.01
adam_eps = 1e-08


def adam_update(param, grad, moment, second):
    new_moment = beta_one * moment + (1.0 - beta_one) * grad
    new_second = beta_two * second + (1.0 - beta_two) * grad * grad
    corrected = new_moment / (1.0 - beta_one**adam_step)
    divisor = jnp.sqrt(new_second / (1.0 - beta_two**adam_step)) + adam_eps
    new_param = param - learn_rate * (corrected / divisor + decay_rate * param)
    return (new_param, new_moment, new_second)


def dequantize(quant_codes, block_scales):
    levels_out = jnp.zeros(quant_codes.shape, jnp.float32)
    for position in range(16):
        levels_out = jnp.where(quant_codes == position, nf4_levels[position], levels_out)
    row_count, col_count = quant_codes.shape
    blocks = block_scales.shape[1]
    scaled = levels_out.reshape(row_count, blocks, col_count // blocks) * block_scales[:, :, None]
    return scaled.reshape(row_count, col_count).astype(jnp.bfloat16)


def right_product(left, right):
    return lax.dot_general(
        left, right, (((1,), (1,)), ((), ())), preferred_element_type=jnp.float32
    )


def left_product(left, right):
    return lax.dot_general(
        left, right, (((0,), (0,)), ((), ())), preferred_element_type=jnp.float32
    )


def add_sources(pieces):
    return (jnp.sum(pieces[0], axis=0, keepdims=True), jnp.sum(pieces[1], axis=0, keepdims=True))


def shards(
    layer_input,
    value_grad,
    quant_codes,
    block_scales,
    tenant_ids,
    live_counts,
    tenant_owner,
    factor_down,
    factor_up,
    moment_down,
    second_down,
    moment_up,
    second_up,
):
    tok_rows, width_part = layer_input.shape
    value_part = value_grad.shape[1]
    slot_count = tenant_ids.shape[0]
    seq_len = tok_rows // slot_count
    tenant_total = tenant_owner.shape[0]
    rank_size = factor_down.shape[1]
    inverse_width = 1.0 / math.sqrt(MODEL_WIDTH)
    coefficient = adapter_scale / math.sqrt(ADAPTER_RANK)
    live_seq = jnp.arange(slot_count, dtype=jnp.int32) < live_counts[0]
    live_tok = jnp.broadcast_to(live_seq[:, None], (slot_count, seq_len)).reshape(tok_rows)
    masked = jnp.where(live_tok[:, None], value_grad, jnp.zeros_like(value_grad))
    tenant_iota = jnp.arange(tenant_total, dtype=jnp.int32)
    matches = tenant_ids[:, None] == tenant_iota[None, :]
    slot_seq = jnp.sum(jnp.where(matches, tenant_owner[None, :], 0), axis=1)
    onehot_seq = (slot_seq[:, None] == tenant_iota[None, :]).astype(jnp.bfloat16)
    weight_local = dequantize(quant_codes, block_scales)
    all_down, all_up = (
        lax.all_gather(factor_down.astype(jnp.bfloat16), "fsdp", axis=0, tiled=True),
        lax.all_gather(factor_up.astype(jnp.bfloat16), "fsdp", axis=0, tiled=True),
    )
    partial_value = right_product(masked, lax.all_gather(weight_local, "fsdp", axis=0, tiled=True))
    base_input_grad = lax.psum_scatter(
        partial_value.astype(jnp.bfloat16), "tensor", scatter_dimension=1, tiled=True
    ).astype(jnp.float32)
    flattened_down = all_down.reshape(tenant_total * rank_size, width_part)
    up_flat = all_up.reshape(tenant_total * rank_size, value_part)
    onehot_tok = jnp.broadcast_to(
        onehot_seq[:, None, :], (slot_count, seq_len, tenant_total)
    ).reshape(tok_rows, tenant_total)
    selector = onehot_tok.astype(jnp.float32)[:, :, None]
    down_scores = right_product(layer_input, flattened_down).reshape(
        tok_rows, tenant_total, rank_size
    )
    up_scores = right_product(masked, up_flat).reshape(tok_rows, tenant_total, rank_size)
    in_part = jnp.sum(down_scores * selector, axis=1) * inverse_width
    grad_part = jnp.sum(up_scores * selector, axis=1) * coefficient
    in_sum, grad_sum = lax.psum((in_part, grad_part), "tensor")
    input_lowrank = in_sum.astype(jnp.bfloat16)
    gradient_lowrank = grad_sum.astype(jnp.bfloat16)
    spread_gradient = (onehot_tok[:, :, None] * gradient_lowrank[:, None, :]).reshape(
        tok_rows, tenant_total * rank_size
    )
    in_spread = (onehot_tok[:, :, None] * input_lowrank[:, None, :]).reshape(
        tok_rows, tenant_total * rank_size
    )
    adapter_input_grad = (
        jnp.dot(spread_gradient, flattened_down, preferred_element_type=jnp.float32) * inverse_width
    )
    down_terms = (left_product(spread_gradient, layer_input) * inverse_width).reshape(
        tenant_total, rank_size, width_part
    )
    up_terms = (left_product(in_spread, masked) * coefficient).reshape(
        tenant_total, rank_size, value_part
    )
    down_gradient, up_gradient = add_sources(
        (
            lax.all_to_all(
                down_terms.astype(jnp.bfloat16), "fsdp", split_axis=0, concat_axis=0, tiled=True
            ).astype(down_terms.dtype),
            lax.all_to_all(
                up_terms.astype(jnp.bfloat16), "fsdp", split_axis=0, concat_axis=0, tiled=True
            ).astype(up_terms.dtype),
        )
    )
    layer_input_gradient = (base_input_grad + adapter_input_grad).astype(jnp.bfloat16)
    new_down, new_moment_down, new_second_down = adam_update(
        factor_down, down_gradient, moment_down, second_down
    )
    new_up, new_moment_up, new_second_up = adam_update(factor_up, up_gradient, moment_up, second_up)
    return (
        layer_input_gradient,
        new_down,
        new_up,
        new_moment_down,
        new_second_down,
        new_moment_up,
        new_second_up,
    )


CHUNKS = 4


def level_tree(codes):
    rows = [jnp.float32(level) for level in nf4_levels]
    for bit in range(4):
        chosen = (codes & (1 << bit)) != 0
        rows = [jnp.where(chosen, rows[2 * n + 1], rows[2 * n]) for n in range(len(rows) // 2)]
    return rows[0]


def fused_kernel(
    fsdp,
    tensor,
    ids_any,
    live_any,
    owner_any,
    x_any,
    dv_any,
    code_any,
    scale_any,
    fd_any,
    fu_any,
    out_ref,
    dg_ref,
    ug_ref,
    ids_ref,
    live_ref,
    owner_ref,
    x_ref,
    dv_ref,
    code_ref,
    scale_ref,
    fd_ref,
    fu_ref,
    in_s,
    fac,
    gsend,
    gy,
    gz,
    grecv,
    dvs,
    part,
    col,
    wgt,
    outs,
    base,
    fac_s,
    fac_f,
    fac_r,
    gy_s,
    gy_r,
    gz_s,
    gz_r,
    dvz_s,
    dvy_s,
    dvx_s,
    dvc_s,
    dv_r,
    part_s,
    part_r,
    col_s,
    col_r,
    wgt_s,
    wgt_r,
    out_s,
    out_r,
):
    f = lax.axis_index("fsdp")
    t = lax.axis_index("tensor")
    z, y = f // 2, f % 2
    x, c = t // 2, t % 2
    pair, odd = z // 2, z % 2
    wide, planes = tensor // 2, fsdp // 2
    tok_rows, width = x_ref.shape
    value = dv_ref.shape[1]
    w_rows = code_ref.shape[0]
    step_rows = w_rows // (2 * CHUNKS)
    rank = fd_ref.shape[1]
    slots = ids_ref.shape[0]
    seq = tok_rows // slots
    flat = fsdp * rank
    inverse_width = 1.0 / math.sqrt(MODEL_WIDTH)
    coefficient = adapter_scale / math.sqrt(ADAPTER_RANK)
    pending = []

    loads = {}
    for n, (name, src, dst) in enumerate(
        (
            ("fd", fd_any, fd_ref),
            ("fu", fu_any, fu_ref),
            ("dv", dv_any, dv_ref),
            ("live", live_any, live_ref),
            ("scale", scale_any, scale_ref),
            ("code", code_any, code_ref),
            ("x", x_any, x_ref),
            ("ids", ids_any, ids_ref),
            ("owner", owner_any, owner_ref),
        )
    ):
        loads[name] = pltpu.make_async_copy(src, dst, in_s.at[n])
        loads[name].start()

    def remote(src, dst, ss, rs, df, dt):
        return pltpu.make_async_remote_copy(
            src_ref=src,
            dst_ref=dst,
            send_sem=ss,
            recv_sem=rs,
            device_id={"fsdp": df, "tensor": dt},
            device_id_type=pl.DeviceIdType.MESH,
        )

    def send(copy, cond=None):
        if cond is None:
            copy.start()
        else:
            pl.when(cond)(copy.start)
        pending.append((copy, cond))

    barrier = pltpu.get_barrier_semaphore()
    greeted = []

    def greet(df, dt):
        pl.semaphore_signal(
            barrier,
            inc=1,
            device_id={"fsdp": df, "tensor": dt},
            device_id_type=pl.DeviceIdType.MESH,
        )
        greeted.append(1)

    for n in range(1, 8):
        near = 2 * pair + (odd + n // 4) % 2
        greet(2 * near + (y + n // 2) % 2, 2 * x + (c + n) % 2)
    for d in range(1, wide):
        for e in range(2):
            greet(2 * (2 * ((pair + d) % wide) + e) + y, t)
            greet(f, 2 * ((x + d) % wide) + e)

    loads["fd"].wait()
    loads["fu"].wait()
    fac[pl.ds(f, 1), :, 0:width] = fd_ref[...].astype(jnp.bfloat16)
    fac[pl.ds(f, 1), :, width : width + value] = fu_ref[...].astype(jnp.bfloat16)
    loads["dv"].wait()
    loads["live"].wait()
    tok_index = lax.broadcasted_iota(jnp.int32, (tok_rows, value), 0)
    masked = jnp.where(
        tok_index < live_ref[0] * seq, dv_ref[...].astype(jnp.float32), 0.0
    ).astype(jnp.bfloat16)
    dvs[t, odd, y] = masked

    def dequant(half, chunk):
        rows = pl.ds((half * CHUNKS + chunk) * step_rows, step_rows)
        levels = level_tree(code_ref[rows, :])
        scales = jnp.transpose(scale_ref[:, rows])
        blocks = scales.shape[1]
        block = value // blocks
        lane = lax.broadcasted_iota(jnp.int32, (step_rows, value), 1)
        spread = jnp.broadcast_to(scales[:, blocks - 1 : blocks], (step_rows, value))
        for n in reversed(range(blocks - 1)):
            spread = jnp.where(lane < (n + 1) * block, scales[:, n : n + 1], spread)
        col[pair, half, chunk] = (levels * spread).astype(jnp.bfloat16)

    pl.semaphore_wait(barrier, len(greeted))

    def fac_copy(dz, source):
        return remote(
            fac.at[source], fac.at[source], fac_s.at[dz], fac_r.at[source], (f + 2 * dz) % fsdp, t
        )

    def fac_forward(dz, source):
        return remote(
            fac.at[source], fac.at[source], fac_f.at[dz], fac_r.at[source], 2 * z + 1 - y, t
        )

    for dz in range(1, planes):
        send(fac_copy(dz, f))
    send(fac_forward(0, f))

    def dv_near(parity, sy):
        ref = dvs.at[t, parity, sy]
        return remote(ref, ref, dvz_s.at[0], dv_r.at[t, parity, sy], 2 * (4 * pair + 1 - z) + y, t)

    def dv_over(n, parity, sy):
        ref = dvs.at[t, parity, sy]
        return remote(ref, ref, dvy_s.at[n], dv_r.at[t, parity, sy], 2 * z + 1 - y, t)

    def dv_along(n, d, st, parity):
        ref = dvs.at[st, parity]
        to = 2 * ((x + d) % wide) + c
        return remote(ref, ref, dvx_s.at[n, d], dv_r.at[st, parity, 0], f, to)

    def dv_core(n, d, st, parity):
        ref = dvs.at[st, parity]
        return remote(ref, ref, dvc_s.at[n, d], dv_r.at[st, parity, 0], f, 2 * x + 1 - c)

    def dv_share(n, parity):
        dv_over(n, parity, 1 - y).wait_recv()
        for d in range(1, wide):
            send(dv_along(n, d, t, parity))
        send(dv_core(n, 0, t, parity))

    send(dv_over(0, odd, y))
    send(dv_near(odd, y))

    def col_copy(d, source, half, chunk):
        ref = col.at[source, half, chunk]
        return remote(
            ref,
            ref,
            col_s.at[d, half, chunk],
            col_r.at[source, half, chunk],
            2 * (2 * ((pair + d) % wide) + odd) + y,
            t,
        )

    def wgt_copy(d, source, half, chunk):
        return remote(
            col.at[source, half, chunk],
            wgt.at[t, chunk],
            wgt_s.at[d, half, chunk],
            wgt_r.at[t, chunk],
            f,
            2 * source + half,
        )

    def hand_out(d, half, chunk):
        source = (pair + d) % wide
        send(wgt_copy(d, source, half, chunk), 2 * source + half != t)

    loads["scale"].wait()
    loads["code"].wait()
    for chunk in range(CHUNKS):
        for half in range(2):
            dequant(half, chunk)
            for d in range(1, wide):
                send(col_copy(d, pair, half, chunk))
            hand_out(0, half, chunk)

    def forward(chunk):
        for d in range(1, wide):
            for half in range(2):
                col_copy(d, (pair + d) % wide, half, chunk).wait_recv()
                hand_out(d, half, chunk)

    for dz in range(1, planes):
        source = (f + 2 * dz) % fsdp
        fac_copy(dz, source).wait_recv()
        send(fac_forward(dz, source))
    dv_share(0, odd)
    dv_near(1 - odd, y).wait_recv()
    send(dv_over(1, 1 - odd, y))

    loads["ids"].wait()
    loads["owner"].wait()
    slot_row = jnp.zeros((1, tok_rows), jnp.int32)
    seq_row = lax.broadcasted_iota(jnp.int32, (1, tok_rows), 1) // seq
    for n in range(slots):
        own = jnp.int32(0)
        for u in range(fsdp):
            own = own + jnp.where(ids_ref[n] == u, owner_ref[u], 0)
        slot_row = jnp.where(seq_row == n, own, slot_row)
    named = lax.broadcasted_iota(jnp.int32, (flat, tok_rows), 0) // rank
    chosen = named == jnp.broadcast_to(slot_row, (flat, tok_rows))

    forward(0)
    for dz in range(planes):
        source = (2 * z + 2 * dz) % fsdp + 1 - y
        fac_forward(dz, source).wait_recv()
    loads["x"].wait()
    all_down = fac[:, :, 0:width].reshape(flat, width)
    all_up = fac[:, :, width : width + value].reshape(flat, value)

    def folded(scores, factor):
        kept = jnp.where(chosen, scores, 0.0).reshape(fsdp, rank, tok_rows)
        return jnp.sum(kept, axis=0) * factor

    part[t, 0:rank, :] = folded(right_product(all_down, x_ref[...]), inverse_width)
    part[t, rank : 2 * rank, :] = folded(right_product(all_up, masked), coefficient)

    def part_copy(dt, source):
        return remote(part.at[source], part.at[source], part_s.at[dt], part_r.at[source], f, dt)

    for step in range(1, tensor):
        send(part_copy((t + step) % tensor, t))

    dv_share(1, 1 - odd)
    forward(1)

    for step in range(1, tensor):
        source = (t + step) % tensor
        part_copy(source, source).wait_recv()
    sums = jnp.sum(part[...], axis=0)
    low = sums.astype(jnp.bfloat16).astype(jnp.float32)

    def spread_out(rows):
        tiled = jnp.broadcast_to(rows[None], (fsdp, rank, tok_rows)).reshape(flat, tok_rows)
        return jnp.where(chosen, tiled, 0.0).astype(jnp.bfloat16)

    in_spread = spread_out(low[0:rank])
    grad_spread = spread_out(low[rank : 2 * rank])
    down_terms = jnp.dot(grad_spread, x_ref[...], preferred_element_type=jnp.float32)
    by_slot = (down_terms * inverse_width).astype(jnp.bfloat16).reshape(fsdp, rank, width)
    up_terms = jnp.dot(in_spread, masked, preferred_element_type=jnp.float32)
    up_slot = (up_terms * coefficient).astype(jnp.bfloat16).reshape(fsdp, rank, value)
    for slot in range(fsdp):
        gsend[slot % 2, slot // 2, :, 0:width] = by_slot[slot]
        gsend[slot % 2, slot // 2, :, width : width + value] = up_slot[slot]
    over = remote(gsend.at[1 - y], gy, gy_s.at[0], gy_r.at[0], 2 * z + 1 - y, t)
    send(over)

    def grad_copy(dz, to, source):
        return remote(
            gz.at[to], grecv.at[source], gz_s.at[dz], gz_r.at[source], (f + 2 * dz) % fsdp, t
        )

    forward(2)
    for n, parity in enumerate((odd, 1 - odd)):
        for d in range(1, wide):
            st = 2 * ((x + d) % wide) + c
            dv_along(n, d, st, parity).wait_recv()
            send(dv_core(n, d, st, parity))
    over.wait_recv()
    gz[...] = (gsend[y].astype(jnp.float32) + gy[...].astype(jnp.float32)).astype(jnp.bfloat16)
    for dz in range(1, planes):
        send(grad_copy(dz, (z + dz) % planes, z))
    grecv[pl.ds(z, 1)] = gz[pl.ds(z, 1)]
    for later in range(3, CHUNKS):
        forward(later)

    for d in range(wide):
        for parity in range(2):
            dv_core(0, 0, 2 * d + 1 - c, parity).wait_recv()

    def multiply(chunk):
        for step in range(1, tensor):
            source = (t + step) % tensor
            arrived = remote(
                col.at[0, 0, chunk],
                wgt.at[source, chunk],
                wgt_s.at[0, 0, chunk],
                wgt_r.at[source, chunk],
                f,
                source,
            )
            arrived.wait_recv()
        rows = 4 * tok_rows
        total = right_product(dvs[t].reshape(rows, value), col[x, c, chunk])
        for step in range(1, tensor):
            source = (t + step) % tensor
            total = total + right_product(dvs[source].reshape(rows, value), wgt[source, chunk])
        for parity in range(2):
            for half in range(2):
                start = (2 * parity + half) * tok_rows
                piece = total[start : start + tok_rows].astype(jnp.bfloat16)
                outs[chunk, parity, half] = piece
                df, dt = 2 * (2 * pair + parity) + half, 2 * x + odd
                stays = jnp.logical_and(df == f, dt == t)

                @pl.when(stays)
                def _(piece=piece):
                    base[y, c, chunk] = piece

                copy = remote(
                    outs.at[chunk, parity, half],
                    base.at[y, c, chunk],
                    out_s.at[chunk, parity, half],
                    out_r.at[y, c, chunk],
                    df,
                    dt,
                )
                send(copy, jnp.logical_not(stays))

    for chunk in range(CHUNKS):
        multiply(chunk)

    for dz in range(1, planes):
        grad_copy(dz, 0, (z + dz) % planes).wait_recv()
    dg_ref[...] = jnp.sum(grecv[:, :, 0:width].astype(jnp.float32), axis=0, keepdims=True)
    ug_ref[...] = jnp.sum(
        grecv[:, :, width : width + value].astype(jnp.float32), axis=0, keepdims=True
    )

    for chunk in range(CHUNKS):
        for half in range(2):
            for core in range(2):
                stays = jnp.logical_and(odd == c, jnp.logical_and(half == y, core == c))
                arrived = remote(
                    outs.at[chunk, 0, 0],
                    base.at[half, core, chunk],
                    out_s.at[chunk, 0, 0],
                    out_r.at[half, core, chunk],
                    f,
                    2 * x + 1 - c,
                )
                pl.when(jnp.logical_not(stays))(arrived.wait_recv)
                start = half * w_rows + (core * CHUNKS + chunk) * step_rows
                low_term = lax.dot_general(
                    grad_spread,
                    fac[:, :, start : start + step_rows].reshape(flat, step_rows),
                    (((0,), (0,)), ((), ())),
                    preferred_element_type=jnp.float32,
                )
                out_ref[:, start : start + step_rows] = (
                    base[half, core, chunk].astype(jnp.float32) + low_term * inverse_width
                ).astype(jnp.bfloat16)

    for copy, cond in pending:
        if cond is None:
            copy.wait_send()
        else:
            pl.when(cond)(copy.wait_send)


def fused(fsdp, tensor, *args):
    (
        layer_input,
        value_grad,
        quant_codes,
        block_scales,
        tenant_ids,
        live_counts,
        tenant_owner,
        factor_down,
        factor_up,
        moment_down,
        second_down,
        moment_up,
        second_up,
    ) = args
    tok_rows, width = layer_input.shape
    value = value_grad.shape[1]
    w_rows = quant_codes.shape[0]
    rank = factor_down.shape[1]
    step_rows = w_rows // (2 * CHUNKS)
    wide, planes = tensor // 2, fsdp // 2
    low = jnp.bfloat16
    dma = pltpu.SemaphoreType.DMA
    vmem = pl.BlockSpec(memory_space=pltpu.VMEM)
    like = jax.ShapeDtypeStruct
    layer_input_gradient, down_gradient, up_gradient = pl.pallas_call(
        functools.partial(fused_kernel, fsdp, tensor),
        out_shape=(
            like(layer_input.shape, low),
            like(factor_down.shape, jnp.float32),
            like(factor_up.shape, jnp.float32),
        ),
        in_specs=[pl.BlockSpec(memory_space=pl.ANY)] * 9,
        out_specs=(vmem,) * 3,
        scratch_shapes=[
            pltpu.SMEM(tenant_ids.shape, jnp.int32),
            pltpu.SMEM(live_counts.shape, jnp.int32),
            pltpu.SMEM(tenant_owner.shape, jnp.int32),
            pltpu.VMEM(layer_input.shape, low),
            pltpu.VMEM(value_grad.shape, low),
            pltpu.VMEM(quant_codes.shape, jnp.int32),
            pltpu.VMEM(block_scales.shape[::-1], jnp.float32),
            pltpu.VMEM(factor_down.shape, jnp.float32),
            pltpu.VMEM(factor_up.shape, jnp.float32),
            dma((9,)),
            pltpu.VMEM((fsdp, rank, width + value), low),
            pltpu.VMEM((2, planes, rank, width + value), low),
            pltpu.VMEM((planes, rank, width + value), low),
            pltpu.VMEM((planes, rank, width + value), low),
            pltpu.VMEM((planes, rank, width + value), low),
            pltpu.VMEM((tensor, 2, 2, tok_rows, value), low),
            pltpu.VMEM((tensor, 2 * rank, tok_rows), jnp.float32),
            pltpu.VMEM((wide, 2, CHUNKS, step_rows, value), low),
            pltpu.VMEM((tensor, CHUNKS, step_rows, value), low),
            pltpu.VMEM((CHUNKS, 2, 2, tok_rows, step_rows), low),
            pltpu.VMEM((2, 2, CHUNKS, tok_rows, step_rows), low),
            dma((planes,)),
            dma((planes,)),
            dma((fsdp,)),
            dma((1,)),
            dma((1,)),
            dma((planes,)),
            dma((planes,)),
            dma((1,)),
            dma((2,)),
            dma((2, wide)),
            dma((2, wide)),
            dma((tensor, 2, 2)),
            dma((tensor,)),
            dma((tensor,)),
            dma((wide, 2, CHUNKS)),
            dma((wide, 2, CHUNKS)),
            dma((wide, 2, CHUNKS)),
            dma((tensor, CHUNKS)),
            dma((CHUNKS, 2, 2)),
            dma((2, 2, CHUNKS)),
        ],
        compiler_params=pltpu.CompilerParams(
            collective_id=0, has_side_effects=True, vmem_limit_bytes=56 * 1024 * 1024
        ),
    )(
        tenant_ids,
        live_counts,
        tenant_owner,
        layer_input,
        value_grad,
        quant_codes,
        block_scales.T,
        factor_down,
        factor_up,
    )
    new_down, new_moment_down, new_second_down = adam_update(
        factor_down, down_gradient, moment_down, second_down
    )
    new_up, new_moment_up, new_second_up = adam_update(factor_up, up_gradient, moment_up, second_up)
    return (
        layer_input_gradient,
        new_down,
        new_up,
        new_moment_down,
        new_second_down,
        new_moment_up,
        new_second_up,
    )


def solution(mesh):
    fsdp, tensor = mesh.shape["fsdp"], mesh.shape["tensor"]
    planar = fsdp == 2 * tensor and tensor % 2 == 0
    body = functools.partial(fused, fsdp, tensor) if planar else shards
    in_specs = (
        P("fsdp", "tensor"),
        P("fsdp", "tensor"),
        P("fsdp", "tensor"),
        P("fsdp", "tensor"),
        P("fsdp"),
        P("fsdp"),
        P(),
        P("fsdp", None, "tensor"),
        P("fsdp", None, "tensor"),
        P("fsdp", None, "tensor"),
        P("fsdp", None, "tensor"),
        P("fsdp", None, "tensor"),
        P("fsdp", None, "tensor"),
    )
    out_specs = (
        P("fsdp", "tensor"),
        P("fsdp", None, "tensor"),
        P("fsdp", None, "tensor"),
        P("fsdp", None, "tensor"),
        P("fsdp", None, "tensor"),
        P("fsdp", None, "tensor"),
        P("fsdp", None, "tensor"),
    )
    return jax.shard_map(body, mesh=mesh, in_specs=in_specs, out_specs=out_specs, check_vma=False)
```

```python
import functools
import math

import jax
import jax.numpy as jnp
from jax import lax
from jax.experimental import pallas as pl
from jax.experimental.pallas import tpu as pltpu
from jax.sharding import PartitionSpec as P

MODEL_WIDTH = 8192
ADAPTER_RANK = 16


nf4_levels = (
    -1.0,
    -0.6962,
    -0.5251,
    -0.3949,
    -0.2844,
    -0.1848,
    -0.0911,
    0.0,
    0.0796,
    0.1609,
    0.2461,
    0.3379,
    0.4407,
    0.5626,
    0.723,
    1.0,
)
adapter_scale = 2.0
beta_one = 0.9
beta_two = 0.999
adam_step = 10.0
learn_rate = 0.05
decay_rate = 0.01
adam_eps = 1e-08


def adam_update(param, grad, moment, second):
    new_moment = beta_one * moment + (1.0 - beta_one) * grad
    new_second = beta_two * second + (1.0 - beta_two) * grad * grad
    corrected = new_moment / (1.0 - beta_one**adam_step)
    divisor = jnp.sqrt(new_second / (1.0 - beta_two**adam_step)) + adam_eps
    new_param = param - learn_rate * (corrected / divisor + decay_rate * param)
    return (new_param, new_moment, new_second)


def dequantize(quant_codes, block_scales):
    levels_out = jnp.zeros(quant_codes.shape, jnp.float32)
    for position in range(16):
        levels_out = jnp.where(quant_codes == position, nf4_levels[position], levels_out)
    row_count, col_count = quant_codes.shape
    blocks = block_scales.shape[1]
    scaled = levels_out.reshape(row_count, blocks, col_count // blocks) * block_scales[:, :, None]
    return scaled.reshape(row_count, col_count).astype(jnp.bfloat16)


def right_product(left, right):
    return lax.dot_general(
        left, right, (((1,), (1,)), ((), ())), preferred_element_type=jnp.float32
    )


def left_product(left, right):
    return lax.dot_general(
        left, right, (((0,), (0,)), ((), ())), preferred_element_type=jnp.float32
    )


def add_sources(pieces):
    return (jnp.sum(pieces[0], axis=0, keepdims=True), jnp.sum(pieces[1], axis=0, keepdims=True))


def shards(
    layer_input,
    value_grad,
    quant_codes,
    block_scales,
    tenant_ids,
    live_counts,
    tenant_owner,
    factor_down,
    factor_up,
    moment_down,
    second_down,
    moment_up,
    second_up,
):
    tok_rows, width_part = layer_input.shape
    value_part = value_grad.shape[1]
    slot_count = tenant_ids.shape[0]
    seq_len = tok_rows // slot_count
    tenant_total = tenant_owner.shape[0]
    rank_size = factor_down.shape[1]
    inverse_width = 1.0 / math.sqrt(MODEL_WIDTH)
    coefficient = adapter_scale / math.sqrt(ADAPTER_RANK)
    live_seq = jnp.arange(slot_count, dtype=jnp.int32) < live_counts[0]
    live_tok = jnp.broadcast_to(live_seq[:, None], (slot_count, seq_len)).reshape(tok_rows)
    masked = jnp.where(live_tok[:, None], value_grad, jnp.zeros_like(value_grad))
    tenant_iota = jnp.arange(tenant_total, dtype=jnp.int32)
    matches = tenant_ids[:, None] == tenant_iota[None, :]
    slot_seq = jnp.sum(jnp.where(matches, tenant_owner[None, :], 0), axis=1)
    onehot_seq = (slot_seq[:, None] == tenant_iota[None, :]).astype(jnp.bfloat16)
    weight_local = dequantize(quant_codes, block_scales)
    all_down, all_up = (
        lax.all_gather(factor_down.astype(jnp.bfloat16), "fsdp", axis=0, tiled=True),
        lax.all_gather(factor_up.astype(jnp.bfloat16), "fsdp", axis=0, tiled=True),
    )
    partial_value = right_product(masked, lax.all_gather(weight_local, "fsdp", axis=0, tiled=True))
    base_input_grad = lax.psum_scatter(
        partial_value.astype(jnp.bfloat16), "tensor", scatter_dimension=1, tiled=True
    ).astype(jnp.float32)
    flattened_down = all_down.reshape(tenant_total * rank_size, width_part)
    up_flat = all_up.reshape(tenant_total * rank_size, value_part)
    onehot_tok = jnp.broadcast_to(
        onehot_seq[:, None, :], (slot_count, seq_len, tenant_total)
    ).reshape(tok_rows, tenant_total)
    selector = onehot_tok.astype(jnp.float32)[:, :, None]
    down_scores = right_product(layer_input, flattened_down).reshape(
        tok_rows, tenant_total, rank_size
    )
    up_scores = right_product(masked, up_flat).reshape(tok_rows, tenant_total, rank_size)
    in_part = jnp.sum(down_scores * selector, axis=1) * inverse_width
    grad_part = jnp.sum(up_scores * selector, axis=1) * coefficient
    in_sum, grad_sum = lax.psum((in_part, grad_part), "tensor")
    input_lowrank = in_sum.astype(jnp.bfloat16)
    gradient_lowrank = grad_sum.astype(jnp.bfloat16)
    spread_gradient = (onehot_tok[:, :, None] * gradient_lowrank[:, None, :]).reshape(
        tok_rows, tenant_total * rank_size
    )
    in_spread = (onehot_tok[:, :, None] * input_lowrank[:, None, :]).reshape(
        tok_rows, tenant_total * rank_size
    )
    adapter_input_grad = (
        jnp.dot(spread_gradient, flattened_down, preferred_element_type=jnp.float32) * inverse_width
    )
    down_terms = (left_product(spread_gradient, layer_input) * inverse_width).reshape(
        tenant_total, rank_size, width_part
    )
    up_terms = (left_product(in_spread, masked) * coefficient).reshape(
        tenant_total, rank_size, value_part
    )
    down_gradient, up_gradient = add_sources(
        (
            lax.all_to_all(
                down_terms.astype(jnp.bfloat16), "fsdp", split_axis=0, concat_axis=0, tiled=True
            ).astype(down_terms.dtype),
            lax.all_to_all(
                up_terms.astype(jnp.bfloat16), "fsdp", split_axis=0, concat_axis=0, tiled=True
            ).astype(up_terms.dtype),
        )
    )
    layer_input_gradient = (base_input_grad + adapter_input_grad).astype(jnp.bfloat16)
    new_down, new_moment_down, new_second_down = adam_update(
        factor_down, down_gradient, moment_down, second_down
    )
    new_up, new_moment_up, new_second_up = adam_update(factor_up, up_gradient, moment_up, second_up)
    return (
        layer_input_gradient,
        new_down,
        new_up,
        new_moment_down,
        new_second_down,
        new_moment_up,
        new_second_up,
    )


CHUNKS = 4


def level_tree(codes):
    rows = [jnp.float32(level) for level in nf4_levels]
    for bit in range(4):
        chosen = (codes & (1 << bit)) != 0
        rows = [jnp.where(chosen, rows[2 * n + 1], rows[2 * n]) for n in range(len(rows) // 2)]
    return rows[0]


def fused_kernel(
    fsdp,
    tensor,
    ids_any,
    live_any,
    owner_any,
    x_any,
    dv_any,
    code_any,
    scale_any,
    fd_any,
    fu_any,
    md_any,
    sd_any,
    mu_any,
    su_any,
    out_ref,
    nd_ref,
    nu_ref,
    nmd_ref,
    nsd_ref,
    nmu_ref,
    nsu_ref,
    ids_ref,
    live_ref,
    owner_ref,
    x_ref,
    dv_ref,
    code_ref,
    scale_ref,
    fd_ref,
    fu_ref,
    md_ref,
    sd_ref,
    mu_ref,
    su_ref,
    in_s,
    fac,
    gsend,
    gy,
    gz,
    grecv,
    dvs,
    part,
    col,
    wgt,
    outs,
    base,
    lows,
    fac_s,
    fac_f,
    fac_r,
    gy_s,
    gy_r,
    gz_s,
    gz_r,
    dvz_s,
    dvy_s,
    dvx_s,
    dvc_s,
    dv_r,
    part_s,
    part_r,
    col_s,
    col_r,
    wgt_s,
    wgt_r,
    out_s,
    out_r,
):
    f = lax.axis_index("fsdp")
    t = lax.axis_index("tensor")
    z, y = f // 2, f % 2
    x, c = t // 2, t % 2
    pair, odd = z // 2, z % 2
    wide, planes = tensor // 2, fsdp // 2
    tok_rows, width = x_ref.shape
    value = dv_ref.shape[1]
    w_rows = code_ref.shape[0]
    step_rows = w_rows // (2 * CHUNKS)
    rank = fd_ref.shape[1]
    slots = ids_ref.shape[0]
    seq = tok_rows // slots
    flat = fsdp * rank
    inverse_width = 1.0 / math.sqrt(MODEL_WIDTH)
    coefficient = adapter_scale / math.sqrt(ADAPTER_RANK)
    pending = []

    loads = {}
    for n, (name, src, dst) in enumerate(
        (
            ("fd", fd_any, fd_ref),
            ("fu", fu_any, fu_ref),
            ("dv", dv_any, dv_ref),
            ("live", live_any, live_ref),
            ("scale", scale_any, scale_ref),
            ("code", code_any, code_ref),
            ("x", x_any, x_ref),
            ("ids", ids_any, ids_ref),
            ("owner", owner_any, owner_ref),
            ("md", md_any, md_ref),
            ("sd", sd_any, sd_ref),
            ("mu", mu_any, mu_ref),
            ("su", su_any, su_ref),
        )
    ):
        loads[name] = pltpu.make_async_copy(src, dst, in_s.at[n])
        loads[name].start()

    def remote(src, dst, ss, rs, df, dt):
        return pltpu.make_async_remote_copy(
            src_ref=src,
            dst_ref=dst,
            send_sem=ss,
            recv_sem=rs,
            device_id={"fsdp": df, "tensor": dt},
            device_id_type=pl.DeviceIdType.MESH,
        )

    def send(copy, cond=None):
        if cond is None:
            copy.start()
        else:
            pl.when(cond)(copy.start)
        pending.append((copy, cond))

    barrier = pltpu.get_barrier_semaphore()
    greeted = []

    def greet(df, dt):
        pl.semaphore_signal(
            barrier,
            inc=1,
            device_id={"fsdp": df, "tensor": dt},
            device_id_type=pl.DeviceIdType.MESH,
        )
        greeted.append(1)

    for n in range(1, 8):
        near = 2 * pair + (odd + n // 4) % 2
        greet(2 * near + (y + n // 2) % 2, 2 * x + (c + n) % 2)
    for d in range(1, wide):
        for e in range(2):
            greet(2 * (2 * ((pair + d) % wide) + e) + y, t)
            greet(f, 2 * ((x + d) % wide) + e)

    loads["fd"].wait()
    loads["fu"].wait()
    fac[pl.ds(f, 1), :, 0:width] = fd_ref[...].astype(jnp.bfloat16)
    fac[pl.ds(f, 1), :, width : width + value] = fu_ref[...].astype(jnp.bfloat16)
    loads["dv"].wait()
    loads["live"].wait()
    tok_index = lax.broadcasted_iota(jnp.int32, (tok_rows, value), 0)
    masked = jnp.where(
        tok_index < live_ref[0] * seq, dv_ref[...].astype(jnp.float32), 0.0
    ).astype(jnp.bfloat16)
    dvs[t, odd, y] = masked

    def dequant(half, chunk):
        rows = pl.ds((half * CHUNKS + chunk) * step_rows, step_rows)
        levels = level_tree(code_ref[rows, :])
        scales = jnp.transpose(scale_ref[:, rows])
        blocks = scales.shape[1]
        block = value // blocks
        lane = lax.broadcasted_iota(jnp.int32, (step_rows, value), 1)
        spread = jnp.broadcast_to(scales[:, blocks - 1 : blocks], (step_rows, value))
        for n in reversed(range(blocks - 1)):
            spread = jnp.where(lane < (n + 1) * block, scales[:, n : n + 1], spread)
        col[pair, half, chunk] = (levels * spread).astype(jnp.bfloat16)

    pl.semaphore_wait(barrier, len(greeted))

    def fac_copy(dz, source):
        return remote(
            fac.at[source], fac.at[source], fac_s.at[dz], fac_r.at[source], (f + 2 * dz) % fsdp, t
        )

    def fac_forward(dz, source):
        return remote(
            fac.at[source], fac.at[source], fac_f.at[dz], fac_r.at[source], 2 * z + 1 - y, t
        )

    for dz in range(1, planes):
        send(fac_copy(dz, f))
    send(fac_forward(0, f))

    def dv_near(parity, sy):
        ref = dvs.at[t, parity, sy]
        return remote(ref, ref, dvz_s.at[0], dv_r.at[t, parity, sy], 2 * (4 * pair + 1 - z) + y, t)

    def dv_over(n, parity, sy):
        ref = dvs.at[t, parity, sy]
        return remote(ref, ref, dvy_s.at[n], dv_r.at[t, parity, sy], 2 * z + 1 - y, t)

    def dv_along(n, d, st, parity):
        ref = dvs.at[st, parity]
        to = 2 * ((x + d) % wide) + c
        return remote(ref, ref, dvx_s.at[n, d], dv_r.at[st, parity, 0], f, to)

    def dv_core(n, d, st, parity):
        ref = dvs.at[st, parity]
        return remote(ref, ref, dvc_s.at[n, d], dv_r.at[st, parity, 0], f, 2 * x + 1 - c)

    def dv_share(n, parity):
        dv_over(n, parity, 1 - y).wait_recv()
        for d in range(1, wide):
            send(dv_along(n, d, t, parity))
        send(dv_core(n, 0, t, parity))

    send(dv_over(0, odd, y))
    send(dv_near(odd, y))

    def col_copy(d, source, half, chunk):
        ref = col.at[source, half, chunk]
        return remote(
            ref,
            ref,
            col_s.at[d, half, chunk],
            col_r.at[source, half, chunk],
            2 * (2 * ((pair + d) % wide) + odd) + y,
            t,
        )

    def wgt_copy(d, source, half, chunk):
        return remote(
            col.at[source, half, chunk],
            wgt.at[t, chunk],
            wgt_s.at[d, half, chunk],
            wgt_r.at[t, chunk],
            f,
            2 * source + half,
        )

    def hand_out(d, half, chunk):
        source = (pair + d) % wide
        send(wgt_copy(d, source, half, chunk), 2 * source + half != t)

    loads["scale"].wait()
    loads["code"].wait()
    for chunk in range(CHUNKS):
        for half in range(2):
            dequant(half, chunk)
            for d in range(1, wide):
                send(col_copy(d, pair, half, chunk))
            hand_out(0, half, chunk)

    def forward(chunk):
        for d in range(1, wide):
            for half in range(2):
                col_copy(d, (pair + d) % wide, half, chunk).wait_recv()
                hand_out(d, half, chunk)

    for dz in range(1, planes):
        source = (f + 2 * dz) % fsdp
        fac_copy(dz, source).wait_recv()
        send(fac_forward(dz, source))
    dv_share(0, odd)
    dv_near(1 - odd, y).wait_recv()
    send(dv_over(1, 1 - odd, y))

    loads["ids"].wait()
    loads["owner"].wait()
    slot_row = jnp.zeros((1, tok_rows), jnp.int32)
    seq_row = lax.broadcasted_iota(jnp.int32, (1, tok_rows), 1) // seq
    for n in range(slots):
        own = jnp.int32(0)
        for u in range(fsdp):
            own = own + jnp.where(ids_ref[n] == u, owner_ref[u], 0)
        slot_row = jnp.where(seq_row == n, own, slot_row)
    named = lax.broadcasted_iota(jnp.int32, (flat, tok_rows), 0) // rank
    chosen = named == jnp.broadcast_to(slot_row, (flat, tok_rows))

    forward(0)
    for dz in range(planes):
        source = (2 * z + 2 * dz) % fsdp + 1 - y
        fac_forward(dz, source).wait_recv()
    loads["x"].wait()
    all_down = fac[:, :, 0:width].reshape(flat, width)
    all_up = fac[:, :, width : width + value].reshape(flat, value)

    def folded(scores, factor):
        kept = jnp.where(chosen, scores, 0.0).reshape(fsdp, rank, tok_rows)
        return jnp.sum(kept, axis=0) * factor

    part[t, 0:rank, :] = folded(right_product(all_down, x_ref[...]), inverse_width)
    part[t, rank : 2 * rank, :] = folded(right_product(all_up, masked), coefficient)

    def part_copy(dt, source):
        return remote(part.at[source], part.at[source], part_s.at[dt], part_r.at[source], f, dt)

    for step in range(1, tensor):
        send(part_copy((t + step) % tensor, t))

    dv_share(1, 1 - odd)
    forward(1)

    for step in range(1, tensor):
        source = (t + step) % tensor
        part_copy(source, source).wait_recv()
    sums = jnp.sum(part[...], axis=0)
    low = sums.astype(jnp.bfloat16).astype(jnp.float32)

    def spread_out(rows):
        tiled = jnp.broadcast_to(rows[None], (fsdp, rank, tok_rows)).reshape(flat, tok_rows)
        return jnp.where(chosen, tiled, 0.0).astype(jnp.bfloat16)

    in_spread = spread_out(low[0:rank])
    grad_spread = spread_out(low[rank : 2 * rank])
    down_terms = jnp.dot(grad_spread, x_ref[...], preferred_element_type=jnp.float32)
    by_slot = (down_terms * inverse_width).astype(jnp.bfloat16).reshape(fsdp, rank, width)
    up_terms = jnp.dot(in_spread, masked, preferred_element_type=jnp.float32)
    up_slot = (up_terms * coefficient).astype(jnp.bfloat16).reshape(fsdp, rank, value)
    for slot in range(fsdp):
        gsend[slot % 2, slot // 2, :, 0:width] = by_slot[slot]
        gsend[slot % 2, slot // 2, :, width : width + value] = up_slot[slot]
    over = remote(gsend.at[1 - y], gy, gy_s.at[0], gy_r.at[0], 2 * z + 1 - y, t)
    send(over)
    lows[...] = inverse_width * lax.dot_general(
        grad_spread, all_down, (((0,), (0,)), ((), ())), preferred_element_type=jnp.float32
    )

    def grad_copy(dz, to, source):
        return remote(
            gz.at[to], grecv.at[source], gz_s.at[dz], gz_r.at[source], (f + 2 * dz) % fsdp, t
        )

    for n, parity in enumerate((odd, 1 - odd)):
        for d in range(1, wide):
            st = 2 * ((x + d) % wide) + c
            dv_along(n, d, st, parity).wait_recv()
            send(dv_core(n, d, st, parity))
    forward(2)
    for d in range(wide):
        for parity in range(2):
            dv_core(0, 0, 2 * d + 1 - c, parity).wait_recv()

    def multiply(chunk):
        for step in range(1, tensor):
            source = (t + step) % tensor
            arrived = remote(
                col.at[0, 0, chunk],
                wgt.at[source, chunk],
                wgt_s.at[0, 0, chunk],
                wgt_r.at[source, chunk],
                f,
                source,
            )
            arrived.wait_recv()
        rows = 4 * tok_rows
        total = right_product(dvs[t].reshape(rows, value), col[x, c, chunk])
        for step in range(1, tensor):
            source = (t + step) % tensor
            total = total + right_product(dvs[source].reshape(rows, value), wgt[source, chunk])
        for parity in range(2):
            for half in range(2):
                start = (2 * parity + half) * tok_rows
                piece = total[start : start + tok_rows].astype(jnp.bfloat16)
                outs[chunk, parity, half] = piece
                df, dt = 2 * (2 * pair + parity) + half, 2 * x + odd
                stays = jnp.logical_and(df == f, dt == t)

                @pl.when(stays)
                def _(piece=piece):
                    base[y, c, chunk] = piece

                copy = remote(
                    outs.at[chunk, parity, half],
                    base.at[y, c, chunk],
                    out_s.at[chunk, parity, half],
                    out_r.at[y, c, chunk],
                    df,
                    dt,
                )
                send(copy, jnp.logical_not(stays))

    multiply(0)
    over.wait_recv()
    gz[...] = (gsend[y].astype(jnp.float32) + gy[...].astype(jnp.float32)).astype(jnp.bfloat16)
    for dz in range(1, planes):
        send(grad_copy(dz, (z + dz) % planes, z))
    grecv[pl.ds(z, 1)] = gz[pl.ds(z, 1)]
    multiply(1)
    multiply(2)
    for later in range(3, CHUNKS):
        forward(later)
        multiply(later)

    for dz in range(1, planes):
        grad_copy(dz, 0, (z + dz) % planes).wait_recv()
    for name in ("md", "sd", "mu", "su"):
        loads[name].wait()
    down_grad = jnp.sum(grecv[:, :, 0:width].astype(jnp.float32), axis=0, keepdims=True)
    up_grad = jnp.sum(
        grecv[:, :, width : width + value].astype(jnp.float32), axis=0, keepdims=True
    )
    nd_ref[...], nmd_ref[...], nsd_ref[...] = adam_update(
        fd_ref[...], down_grad, md_ref[...], sd_ref[...]
    )
    nu_ref[...], nmu_ref[...], nsu_ref[...] = adam_update(
        fu_ref[...], up_grad, mu_ref[...], su_ref[...]
    )

    for chunk in range(CHUNKS):
        for half in range(2):
            for core in range(2):
                stays = jnp.logical_and(odd == c, jnp.logical_and(half == y, core == c))
                arrived = remote(
                    outs.at[chunk, 0, 0],
                    base.at[half, core, chunk],
                    out_s.at[chunk, 0, 0],
                    out_r.at[half, core, chunk],
                    f,
                    2 * x + 1 - c,
                )
                pl.when(jnp.logical_not(stays))(arrived.wait_recv)
                start = half * w_rows + (core * CHUNKS + chunk) * step_rows
                stop = start + step_rows
                out_ref[:, start:stop] = (
                    base[half, core, chunk].astype(jnp.float32) + lows[:, start:stop]
                ).astype(jnp.bfloat16)

    for copy, cond in pending:
        if cond is None:
            copy.wait_send()
        else:
            pl.when(cond)(copy.wait_send)


def write_kernel(count, *refs):
    copies = [
        pltpu.make_async_copy(refs[n], refs[count + n], refs[2 * count].at[n]) for n in range(count)
    ]
    for copy in copies:
        copy.start()
    for copy in copies:
        copy.wait()


def fused(fsdp, tensor, *args):
    (
        layer_input,
        value_grad,
        quant_codes,
        block_scales,
        tenant_ids,
        live_counts,
        tenant_owner,
        factor_down,
        factor_up,
        moment_down,
        second_down,
        moment_up,
        second_up,
    ) = args
    tok_rows, width = layer_input.shape
    value = value_grad.shape[1]
    w_rows = quant_codes.shape[0]
    rank = factor_down.shape[1]
    step_rows = w_rows // (2 * CHUNKS)
    wide, planes = tensor // 2, fsdp // 2
    low = jnp.bfloat16
    dma = pltpu.SemaphoreType.DMA
    vmem = pl.BlockSpec(memory_space=pltpu.VMEM)
    like = jax.ShapeDtypeStruct
    shapes = (
        like(layer_input.shape, low),
        like(factor_down.shape, jnp.float32),
        like(factor_up.shape, jnp.float32),
        like(factor_down.shape, jnp.float32),
        like(factor_down.shape, jnp.float32),
        like(factor_up.shape, jnp.float32),
        like(factor_up.shape, jnp.float32),
    )
    anywhere = pl.BlockSpec(memory_space=pl.ANY)
    results = pl.pallas_call(
        functools.partial(fused_kernel, fsdp, tensor),
        out_shape=shapes,
        in_specs=[anywhere] * 13,
        out_specs=(vmem,) * 7,
        scratch_shapes=[
            pltpu.SMEM(tenant_ids.shape, jnp.int32),
            pltpu.SMEM(live_counts.shape, jnp.int32),
            pltpu.SMEM(tenant_owner.shape, jnp.int32),
            pltpu.VMEM(layer_input.shape, low),
            pltpu.VMEM(value_grad.shape, low),
            pltpu.VMEM(quant_codes.shape, jnp.int32),
            pltpu.VMEM(block_scales.shape[::-1], jnp.float32),
            pltpu.VMEM(factor_down.shape, jnp.float32),
            pltpu.VMEM(factor_up.shape, jnp.float32),
            pltpu.VMEM(moment_down.shape, jnp.float32),
            pltpu.VMEM(second_down.shape, jnp.float32),
            pltpu.VMEM(moment_up.shape, jnp.float32),
            pltpu.VMEM(second_up.shape, jnp.float32),
            dma((13,)),
            pltpu.VMEM((fsdp, rank, width + value), low),
            pltpu.VMEM((2, planes, rank, width + value), low),
            pltpu.VMEM((planes, rank, width + value), low),
            pltpu.VMEM((planes, rank, width + value), low),
            pltpu.VMEM((planes, rank, width + value), low),
            pltpu.VMEM((tensor, 2, 2, tok_rows, value), low),
            pltpu.VMEM((tensor, 2 * rank, tok_rows), jnp.float32),
            pltpu.VMEM((wide, 2, CHUNKS, step_rows, value), low),
            pltpu.VMEM((tensor, CHUNKS, step_rows, value), low),
            pltpu.VMEM((CHUNKS, 2, 2, tok_rows, step_rows), low),
            pltpu.VMEM((2, 2, CHUNKS, tok_rows, step_rows), low),
            pltpu.VMEM((tok_rows, width), jnp.float32),
            dma((planes,)),
            dma((planes,)),
            dma((fsdp,)),
            dma((1,)),
            dma((1,)),
            dma((planes,)),
            dma((planes,)),
            dma((1,)),
            dma((2,)),
            dma((2, wide)),
            dma((2, wide)),
            dma((tensor, 2, 2)),
            dma((tensor,)),
            dma((tensor,)),
            dma((wide, 2, CHUNKS)),
            dma((wide, 2, CHUNKS)),
            dma((wide, 2, CHUNKS)),
            dma((tensor, CHUNKS)),
            dma((CHUNKS, 2, 2)),
            dma((2, 2, CHUNKS)),
        ],
        compiler_params=pltpu.CompilerParams(
            collective_id=0, has_side_effects=True, vmem_limit_bytes=60 * 1024 * 1024
        ),
    )(
        tenant_ids,
        live_counts,
        tenant_owner,
        layer_input,
        value_grad,
        quant_codes,
        block_scales.T,
        factor_down,
        factor_up,
        moment_down,
        second_down,
        moment_up,
        second_up,
    )
    return pl.pallas_call(
        functools.partial(write_kernel, len(shapes)),
        out_shape=shapes,
        in_specs=[anywhere] * len(shapes),
        out_specs=(anywhere,) * len(shapes),
        scratch_shapes=[dma((len(shapes),))],
        compiler_params=pltpu.CompilerParams(vmem_limit_bytes=60 * 1024 * 1024),
    )(*results)


def solution(mesh):
    fsdp, tensor = mesh.shape["fsdp"], mesh.shape["tensor"]
    planar = fsdp == 2 * tensor and tensor % 2 == 0
    body = functools.partial(fused, fsdp, tensor) if planar else shards
    in_specs = (
        P("fsdp", "tensor"),
        P("fsdp", "tensor"),
        P("fsdp", "tensor"),
        P("fsdp", "tensor"),
        P("fsdp"),
        P("fsdp"),
        P(),
        P("fsdp", None, "tensor"),
        P("fsdp", None, "tensor"),
        P("fsdp", None, "tensor"),
        P("fsdp", None, "tensor"),
        P("fsdp", None, "tensor"),
        P("fsdp", None, "tensor"),
    )
    out_specs = (
        P("fsdp", "tensor"),
        P("fsdp", None, "tensor"),
        P("fsdp", None, "tensor"),
        P("fsdp", None, "tensor"),
        P("fsdp", None, "tensor"),
        P("fsdp", None, "tensor"),
        P("fsdp", None, "tensor"),
    )
    return jax.shard_map(body, mesh=mesh, in_specs=in_specs, out_specs=out_specs, check_vma=False)
```

```python
import functools
import math

import jax
import jax.numpy as jnp
from jax import lax
from jax.experimental import pallas as pl
from jax.experimental.pallas import tpu as pltpu
from jax.sharding import PartitionSpec as P

MODEL_WIDTH = 8192
ADAPTER_RANK = 16


nf4_levels = (
    -1.0,
    -0.6962,
    -0.5251,
    -0.3949,
    -0.2844,
    -0.1848,
    -0.0911,
    0.0,
    0.0796,
    0.1609,
    0.2461,
    0.3379,
    0.4407,
    0.5626,
    0.723,
    1.0,
)
adapter_scale = 2.0
beta_one = 0.9
beta_two = 0.999
adam_step = 10.0
learn_rate = 0.05
decay_rate = 0.01
adam_eps = 1e-08


def adam_update(param, grad, moment, second):
    new_moment = beta_one * moment + (1.0 - beta_one) * grad
    new_second = beta_two * second + (1.0 - beta_two) * grad * grad
    corrected = new_moment / (1.0 - beta_one**adam_step)
    divisor = jnp.sqrt(new_second / (1.0 - beta_two**adam_step)) + adam_eps
    new_param = param - learn_rate * (corrected / divisor + decay_rate * param)
    return (new_param, new_moment, new_second)


def dequantize(quant_codes, block_scales):
    levels_out = jnp.zeros(quant_codes.shape, jnp.float32)
    for position in range(16):
        levels_out = jnp.where(quant_codes == position, nf4_levels[position], levels_out)
    row_count, col_count = quant_codes.shape
    blocks = block_scales.shape[1]
    scaled = levels_out.reshape(row_count, blocks, col_count // blocks) * block_scales[:, :, None]
    return scaled.reshape(row_count, col_count).astype(jnp.bfloat16)


def right_product(left, right):
    return lax.dot_general(
        left, right, (((1,), (1,)), ((), ())), preferred_element_type=jnp.float32
    )


def left_product(left, right):
    return lax.dot_general(
        left, right, (((0,), (0,)), ((), ())), preferred_element_type=jnp.float32
    )


def add_sources(pieces):
    return (jnp.sum(pieces[0], axis=0, keepdims=True), jnp.sum(pieces[1], axis=0, keepdims=True))


def shards(
    layer_input,
    value_grad,
    quant_codes,
    block_scales,
    tenant_ids,
    live_counts,
    tenant_owner,
    factor_down,
    factor_up,
    moment_down,
    second_down,
    moment_up,
    second_up,
):
    tok_rows, width_part = layer_input.shape
    value_part = value_grad.shape[1]
    slot_count = tenant_ids.shape[0]
    seq_len = tok_rows // slot_count
    tenant_total = tenant_owner.shape[0]
    rank_size = factor_down.shape[1]
    inverse_width = 1.0 / math.sqrt(MODEL_WIDTH)
    coefficient = adapter_scale / math.sqrt(ADAPTER_RANK)
    live_seq = jnp.arange(slot_count, dtype=jnp.int32) < live_counts[0]
    live_tok = jnp.broadcast_to(live_seq[:, None], (slot_count, seq_len)).reshape(tok_rows)
    masked = jnp.where(live_tok[:, None], value_grad, jnp.zeros_like(value_grad))
    tenant_iota = jnp.arange(tenant_total, dtype=jnp.int32)
    matches = tenant_ids[:, None] == tenant_iota[None, :]
    slot_seq = jnp.sum(jnp.where(matches, tenant_owner[None, :], 0), axis=1)
    onehot_seq = (slot_seq[:, None] == tenant_iota[None, :]).astype(jnp.bfloat16)
    weight_local = dequantize(quant_codes, block_scales)
    all_down, all_up = (
        lax.all_gather(factor_down.astype(jnp.bfloat16), "fsdp", axis=0, tiled=True),
        lax.all_gather(factor_up.astype(jnp.bfloat16), "fsdp", axis=0, tiled=True),
    )
    partial_value = right_product(masked, lax.all_gather(weight_local, "fsdp", axis=0, tiled=True))
    base_input_grad = lax.psum_scatter(
        partial_value.astype(jnp.bfloat16), "tensor", scatter_dimension=1, tiled=True
    ).astype(jnp.float32)
    flattened_down = all_down.reshape(tenant_total * rank_size, width_part)
    up_flat = all_up.reshape(tenant_total * rank_size, value_part)
    onehot_tok = jnp.broadcast_to(
        onehot_seq[:, None, :], (slot_count, seq_len, tenant_total)
    ).reshape(tok_rows, tenant_total)
    selector = onehot_tok.astype(jnp.float32)[:, :, None]
    down_scores = right_product(layer_input, flattened_down).reshape(
        tok_rows, tenant_total, rank_size
    )
    up_scores = right_product(masked, up_flat).reshape(tok_rows, tenant_total, rank_size)
    in_part = jnp.sum(down_scores * selector, axis=1) * inverse_width
    grad_part = jnp.sum(up_scores * selector, axis=1) * coefficient
    in_sum, grad_sum = lax.psum((in_part, grad_part), "tensor")
    input_lowrank = in_sum.astype(jnp.bfloat16)
    gradient_lowrank = grad_sum.astype(jnp.bfloat16)
    spread_gradient = (onehot_tok[:, :, None] * gradient_lowrank[:, None, :]).reshape(
        tok_rows, tenant_total * rank_size
    )
    in_spread = (onehot_tok[:, :, None] * input_lowrank[:, None, :]).reshape(
        tok_rows, tenant_total * rank_size
    )
    adapter_input_grad = (
        jnp.dot(spread_gradient, flattened_down, preferred_element_type=jnp.float32) * inverse_width
    )
    down_terms = (left_product(spread_gradient, layer_input) * inverse_width).reshape(
        tenant_total, rank_size, width_part
    )
    up_terms = (left_product(in_spread, masked) * coefficient).reshape(
        tenant_total, rank_size, value_part
    )
    down_gradient, up_gradient = add_sources(
        (
            lax.all_to_all(
                down_terms.astype(jnp.bfloat16), "fsdp", split_axis=0, concat_axis=0, tiled=True
            ).astype(down_terms.dtype),
            lax.all_to_all(
                up_terms.astype(jnp.bfloat16), "fsdp", split_axis=0, concat_axis=0, tiled=True
            ).astype(up_terms.dtype),
        )
    )
    layer_input_gradient = (base_input_grad + adapter_input_grad).astype(jnp.bfloat16)
    new_down, new_moment_down, new_second_down = adam_update(
        factor_down, down_gradient, moment_down, second_down
    )
    new_up, new_moment_up, new_second_up = adam_update(factor_up, up_gradient, moment_up, second_up)
    return (
        layer_input_gradient,
        new_down,
        new_up,
        new_moment_down,
        new_second_down,
        new_moment_up,
        new_second_up,
    )


CHUNKS = 4


def level_tree(codes):
    rows = [jnp.float32(level) for level in nf4_levels]
    for bit in range(4):
        chosen = (codes & (1 << bit)) != 0
        rows = [jnp.where(chosen, rows[2 * n + 1], rows[2 * n]) for n in range(len(rows) // 2)]
    return rows[0]


def fused_kernel(
    fsdp,
    tensor,
    ids_any,
    live_any,
    owner_any,
    x_any,
    dv_any,
    code_any,
    scale_any,
    fd_any,
    fu_any,
    md_any,
    sd_any,
    mu_any,
    su_any,
    out_ref,
    nd_ref,
    nu_ref,
    nmd_ref,
    nsd_ref,
    nmu_ref,
    nsu_ref,
    ids_ref,
    live_ref,
    owner_ref,
    x_ref,
    dv_ref,
    code_ref,
    scale_ref,
    fd_ref,
    fu_ref,
    md_ref,
    sd_ref,
    mu_ref,
    su_ref,
    in_s,
    fac,
    gsend,
    gy,
    gz,
    grecv,
    dvs,
    part,
    col,
    wgt,
    outs,
    base,
    lows,
    fac_s,
    fac_f,
    fac_r,
    gy_s,
    gy_r,
    gz_s,
    gz_r,
    dvz_s,
    dvy_s,
    dvx_s,
    dvc_s,
    dv_r,
    part_s,
    part_r,
    col_s,
    col_r,
    wgt_s,
    wgt_r,
    out_s,
    out_r,
):
    f = lax.axis_index("fsdp")
    t = lax.axis_index("tensor")
    z, y = f // 2, f % 2
    x, c = t // 2, t % 2
    pair, odd = z // 2, z % 2
    wide, planes = tensor // 2, fsdp // 2
    tok_rows, width = x_ref.shape
    value = dv_ref.shape[1]
    w_rows = code_ref.shape[0]
    step_rows = w_rows // (2 * CHUNKS)
    rank = fd_ref.shape[1]
    slots = ids_ref.shape[0]
    seq = tok_rows // slots
    flat = fsdp * rank
    inverse_width = 1.0 / math.sqrt(MODEL_WIDTH)
    coefficient = adapter_scale / math.sqrt(ADAPTER_RANK)
    pending = []

    loads = {}
    for n, (name, src, dst) in enumerate(
        (
            ("fd", fd_any, fd_ref),
            ("fu", fu_any, fu_ref),
            ("dv", dv_any, dv_ref),
            ("live", live_any, live_ref),
            ("scale", scale_any, scale_ref),
            ("code", code_any, code_ref),
            ("x", x_any, x_ref),
            ("ids", ids_any, ids_ref),
            ("owner", owner_any, owner_ref),
            ("md", md_any, md_ref),
            ("sd", sd_any, sd_ref),
            ("mu", mu_any, mu_ref),
            ("su", su_any, su_ref),
        )
    ):
        loads[name] = pltpu.make_async_copy(src, dst, in_s.at[n])
        loads[name].start()

    def remote(src, dst, ss, rs, df, dt):
        return pltpu.make_async_remote_copy(
            src_ref=src,
            dst_ref=dst,
            send_sem=ss,
            recv_sem=rs,
            device_id={"fsdp": df, "tensor": dt},
            device_id_type=pl.DeviceIdType.MESH,
        )

    def send(copy, cond=None):
        if cond is None:
            copy.start()
        else:
            pl.when(cond)(copy.start)
        pending.append((copy, cond))

    barrier = pltpu.get_barrier_semaphore()
    greeted = []

    def greet(df, dt):
        pl.semaphore_signal(
            barrier,
            inc=1,
            device_id={"fsdp": df, "tensor": dt},
            device_id_type=pl.DeviceIdType.MESH,
        )
        greeted.append(1)

    for n in range(1, 8):
        near = 2 * pair + (odd + n // 4) % 2
        greet(2 * near + (y + n // 2) % 2, 2 * x + (c + n) % 2)
    for d in range(1, wide):
        for e in range(2):
            greet(2 * (2 * ((pair + d) % wide) + e) + y, t)
            greet(f, 2 * ((x + d) % wide) + e)

    loads["fd"].wait()
    loads["fu"].wait()
    fac[pl.ds(f, 1), :, 0:width] = fd_ref[...].astype(jnp.bfloat16)
    fac[pl.ds(f, 1), :, width : width + value] = fu_ref[...].astype(jnp.bfloat16)
    loads["dv"].wait()
    loads["live"].wait()
    tok_index = lax.broadcasted_iota(jnp.int32, (tok_rows, value), 0)
    masked = jnp.where(
        tok_index < live_ref[0] * seq, dv_ref[...].astype(jnp.float32), 0.0
    ).astype(jnp.bfloat16)
    dvs[t, odd, y] = masked

    def dequant(half, chunk):
        rows = pl.ds((half * CHUNKS + chunk) * step_rows, step_rows)
        levels = level_tree(code_ref[rows, :])
        scales = jnp.transpose(scale_ref[:, rows])
        blocks = scales.shape[1]
        block = value // blocks
        lane = lax.broadcasted_iota(jnp.int32, (step_rows, value), 1)
        spread = jnp.broadcast_to(scales[:, blocks - 1 : blocks], (step_rows, value))
        for n in reversed(range(blocks - 1)):
            spread = jnp.where(lane < (n + 1) * block, scales[:, n : n + 1], spread)
        col[pair, half, chunk] = (levels * spread).astype(jnp.bfloat16)

    pl.semaphore_wait(barrier, len(greeted))

    def fac_copy(dz, source):
        return remote(
            fac.at[source], fac.at[source], fac_s.at[dz], fac_r.at[source], (f + 2 * dz) % fsdp, t
        )

    def fac_forward(dz, source):
        return remote(
            fac.at[source], fac.at[source], fac_f.at[dz], fac_r.at[source], 2 * z + 1 - y, t
        )

    for dz in range(1, planes):
        send(fac_copy(dz, f))
    send(fac_forward(0, f))

    def dv_near(parity, sy):
        ref = dvs.at[t, parity, sy]
        return remote(ref, ref, dvz_s.at[0], dv_r.at[t, parity, sy], 2 * (4 * pair + 1 - z) + y, t)

    def dv_over(n, parity, sy):
        ref = dvs.at[t, parity, sy]
        return remote(ref, ref, dvy_s.at[n], dv_r.at[t, parity, sy], 2 * z + 1 - y, t)

    def dv_along(n, d, st, parity, sy):
        ref = dvs.at[st, parity, sy]
        to = 2 * ((x + d) % wide) + c
        return remote(ref, ref, dvx_s.at[n, d], dv_r.at[st, parity, sy], f, to)

    def dv_core(n, d, st, parity, sy):
        ref = dvs.at[st, parity, sy]
        return remote(ref, ref, dvc_s.at[n, d], dv_r.at[st, parity, sy], f, 2 * x + 1 - c)

    def dv_share(n, parity, sy):
        for d in range(1, wide):
            send(dv_along(n, d, t, parity, sy))
        send(dv_core(n, 0, t, parity, sy))

    send(dv_near(odd, y))
    send(dv_over(0, odd, y))
    dv_share(0, odd, y)

    def col_copy(d, source, half, chunk):
        ref = col.at[source, half, chunk]
        return remote(
            ref,
            ref,
            col_s.at[d, half, chunk],
            col_r.at[source, half, chunk],
            2 * (2 * ((pair + d) % wide) + odd) + y,
            t,
        )

    def wgt_copy(d, source, half, chunk):
        return remote(
            col.at[source, half, chunk],
            wgt.at[t, chunk],
            wgt_s.at[d, half, chunk],
            wgt_r.at[t, chunk],
            f,
            2 * source + half,
        )

    def hand_out(d, half, chunk):
        source = (pair + d) % wide
        send(wgt_copy(d, source, half, chunk), 2 * source + half != t)

    loads["scale"].wait()
    loads["code"].wait()
    for chunk in range(CHUNKS):
        for half in range(2):
            dequant(half, chunk)
            for d in range(1, wide):
                send(col_copy(d, pair, half, chunk))

    def forward(chunk):
        for d in range(1, wide):
            for half in range(2):
                col_copy(d, (pair + d) % wide, half, chunk).wait_recv()
                hand_out(d, half, chunk)

    def give(chunk):
        for half in range(2):
            hand_out(0, half, chunk)

    give(0)
    dv_over(0, odd, 1 - y).wait_recv()
    dv_share(1, odd, 1 - y)
    for dz in range(1, planes):
        source = (f + 2 * dz) % fsdp
        fac_copy(dz, source).wait_recv()
        send(fac_forward(dz, source))
    dv_near(1 - odd, y).wait_recv()
    send(dv_over(1, 1 - odd, y))
    dv_share(2, 1 - odd, y)
    give(1)
    dv_over(1, 1 - odd, 1 - y).wait_recv()
    dv_share(3, 1 - odd, 1 - y)
    for later in range(2, CHUNKS):
        give(later)

    loads["ids"].wait()
    loads["owner"].wait()
    slot_row = jnp.zeros((1, tok_rows), jnp.int32)
    seq_row = lax.broadcasted_iota(jnp.int32, (1, tok_rows), 1) // seq
    for n in range(slots):
        own = jnp.int32(0)
        for u in range(fsdp):
            own = own + jnp.where(ids_ref[n] == u, owner_ref[u], 0)
        slot_row = jnp.where(seq_row == n, own, slot_row)
    named = lax.broadcasted_iota(jnp.int32, (flat, tok_rows), 0) // rank
    chosen = named == jnp.broadcast_to(slot_row, (flat, tok_rows))

    forward(0)
    for dz in range(planes):
        source = (2 * z + 2 * dz) % fsdp + 1 - y
        fac_forward(dz, source).wait_recv()
    loads["x"].wait()
    all_down = fac[:, :, 0:width].reshape(flat, width)
    all_up = fac[:, :, width : width + value].reshape(flat, value)

    def folded(scores, factor):
        kept = jnp.where(chosen, scores, 0.0).reshape(fsdp, rank, tok_rows)
        return jnp.sum(kept, axis=0) * factor

    part[t, 0:rank, :] = folded(right_product(all_down, x_ref[...]), inverse_width)
    part[t, rank : 2 * rank, :] = folded(right_product(all_up, masked), coefficient)

    def part_copy(dt, source):
        return remote(part.at[source], part.at[source], part_s.at[dt], part_r.at[source], f, dt)

    for step in range(1, tensor):
        send(part_copy((t + step) % tensor, t))

    for n, (parity, sy) in enumerate(
        ((odd, y), (odd, 1 - y), (1 - odd, y), (1 - odd, 1 - y))
    ):
        for d in range(1, wide):
            st = 2 * ((x + d) % wide) + c
            dv_along(n, d, st, parity, sy).wait_recv()
            send(dv_core(n, d, st, parity, sy))
    forward(1)

    for d in range(wide):
        for parity in range(2):
            for sy in range(2):
                dv_core(0, 0, 2 * d + 1 - c, parity, sy).wait_recv()

    def multiply(chunk):
        for step in range(1, tensor):
            source = (t + step) % tensor
            arrived = remote(
                col.at[0, 0, chunk],
                wgt.at[source, chunk],
                wgt_s.at[0, 0, chunk],
                wgt_r.at[source, chunk],
                f,
                source,
            )
            arrived.wait_recv()
        rows = 4 * tok_rows
        total = right_product(dvs[t].reshape(rows, value), col[x, c, chunk])
        for step in range(1, tensor):
            source = (t + step) % tensor
            total = total + right_product(dvs[source].reshape(rows, value), wgt[source, chunk])
        for parity in range(2):
            for half in range(2):
                start = (2 * parity + half) * tok_rows
                piece = total[start : start + tok_rows].astype(jnp.bfloat16)
                outs[chunk, parity, half] = piece
                df, dt = 2 * (2 * pair + parity) + half, 2 * x + odd
                stays = jnp.logical_and(df == f, dt == t)

                @pl.when(stays)
                def _(piece=piece):
                    base[y, c, chunk] = piece

                copy = remote(
                    outs.at[chunk, parity, half],
                    base.at[y, c, chunk],
                    out_s.at[chunk, parity, half],
                    out_r.at[y, c, chunk],
                    df,
                    dt,
                )
                send(copy, jnp.logical_not(stays))

    multiply(0)

    for step in range(1, tensor):
        source = (t + step) % tensor
        part_copy(source, source).wait_recv()
    sums = jnp.sum(part[...], axis=0)
    low = sums.astype(jnp.bfloat16).astype(jnp.float32)

    def spread_out(rows):
        tiled = jnp.broadcast_to(rows[None], (fsdp, rank, tok_rows)).reshape(flat, tok_rows)
        return jnp.where(chosen, tiled, 0.0).astype(jnp.bfloat16)

    in_spread = spread_out(low[0:rank])
    grad_spread = spread_out(low[rank : 2 * rank])
    down_terms = jnp.dot(grad_spread, x_ref[...], preferred_element_type=jnp.float32)
    by_slot = (down_terms * inverse_width).astype(jnp.bfloat16).reshape(fsdp, rank, width)
    up_terms = jnp.dot(in_spread, masked, preferred_element_type=jnp.float32)
    up_slot = (up_terms * coefficient).astype(jnp.bfloat16).reshape(fsdp, rank, value)
    for slot in range(fsdp):
        gsend[slot % 2, slot // 2, :, 0:width] = by_slot[slot]
        gsend[slot % 2, slot // 2, :, width : width + value] = up_slot[slot]
    over = remote(gsend.at[1 - y], gy, gy_s.at[0], gy_r.at[0], 2 * z + 1 - y, t)
    send(over)

    def grad_copy(dz, to, source):
        return remote(
            gz.at[to], grecv.at[source], gz_s.at[dz], gz_r.at[source], (f + 2 * dz) % fsdp, t
        )

    multiply(1)
    forward(2)
    over.wait_recv()
    gz[...] = (gsend[y].astype(jnp.float32) + gy[...].astype(jnp.float32)).astype(jnp.bfloat16)
    for dz in range(1, planes):
        send(grad_copy(dz, (z + dz) % planes, z))
    grecv[pl.ds(z, 1)] = gz[pl.ds(z, 1)]
    multiply(2)
    lows[...] = inverse_width * lax.dot_general(
        grad_spread, all_down, (((0,), (0,)), ((), ())), preferred_element_type=jnp.float32
    )
    for later in range(3, CHUNKS):
        forward(later)
        multiply(later)

    for dz in range(1, planes):
        grad_copy(dz, 0, (z + dz) % planes).wait_recv()
    for name in ("md", "sd", "mu", "su"):
        loads[name].wait()
    down_grad = jnp.sum(grecv[:, :, 0:width].astype(jnp.float32), axis=0, keepdims=True)
    up_grad = jnp.sum(
        grecv[:, :, width : width + value].astype(jnp.float32), axis=0, keepdims=True
    )
    nd_ref[...], nmd_ref[...], nsd_ref[...] = adam_update(
        fd_ref[...], down_grad, md_ref[...], sd_ref[...]
    )
    nu_ref[...], nmu_ref[...], nsu_ref[...] = adam_update(
        fu_ref[...], up_grad, mu_ref[...], su_ref[...]
    )

    for chunk in range(CHUNKS):
        for half in range(2):
            for core in range(2):
                stays = jnp.logical_and(odd == c, jnp.logical_and(half == y, core == c))
                arrived = remote(
                    outs.at[chunk, 0, 0],
                    base.at[half, core, chunk],
                    out_s.at[chunk, 0, 0],
                    out_r.at[half, core, chunk],
                    f,
                    2 * x + 1 - c,
                )
                pl.when(jnp.logical_not(stays))(arrived.wait_recv)
                start = half * w_rows + (core * CHUNKS + chunk) * step_rows
                stop = start + step_rows
                out_ref[:, start:stop] = (
                    base[half, core, chunk].astype(jnp.float32) + lows[:, start:stop]
                ).astype(jnp.bfloat16)

    for copy, cond in pending:
        if cond is None:
            copy.wait_send()
        else:
            pl.when(cond)(copy.wait_send)


def write_kernel(count, *refs):
    held, sems = refs[2 * count : 3 * count], refs[3 * count]
    loads = [pltpu.make_async_copy(refs[n], held[n], sems.at[0, n]) for n in range(count)]
    stores = [pltpu.make_async_copy(held[n], refs[count + n], sems.at[1, n]) for n in range(count)]
    for load in loads:
        load.start()
    for load, store in zip(loads, stores):
        load.wait()
        store.start()
    for store in stores:
        store.wait()


def fused(fsdp, tensor, *args):
    (
        layer_input,
        value_grad,
        quant_codes,
        block_scales,
        tenant_ids,
        live_counts,
        tenant_owner,
        factor_down,
        factor_up,
        moment_down,
        second_down,
        moment_up,
        second_up,
    ) = args
    tok_rows, width = layer_input.shape
    value = value_grad.shape[1]
    w_rows = quant_codes.shape[0]
    rank = factor_down.shape[1]
    step_rows = w_rows // (2 * CHUNKS)
    wide, planes = tensor // 2, fsdp // 2
    low = jnp.bfloat16
    dma = pltpu.SemaphoreType.DMA
    vmem = pl.BlockSpec(memory_space=pltpu.VMEM)
    like = jax.ShapeDtypeStruct
    shapes = (
        like(layer_input.shape, low),
        like(factor_down.shape, jnp.float32),
        like(factor_up.shape, jnp.float32),
        like(factor_down.shape, jnp.float32),
        like(factor_down.shape, jnp.float32),
        like(factor_up.shape, jnp.float32),
        like(factor_up.shape, jnp.float32),
    )
    anywhere = pl.BlockSpec(memory_space=pl.ANY)
    results = pl.pallas_call(
        functools.partial(fused_kernel, fsdp, tensor),
        out_shape=shapes,
        in_specs=[anywhere] * 13,
        out_specs=(vmem,) * 7,
        scratch_shapes=[
            pltpu.SMEM(tenant_ids.shape, jnp.int32),
            pltpu.SMEM(live_counts.shape, jnp.int32),
            pltpu.SMEM(tenant_owner.shape, jnp.int32),
            pltpu.VMEM(layer_input.shape, low),
            pltpu.VMEM(value_grad.shape, low),
            pltpu.VMEM(quant_codes.shape, jnp.int32),
            pltpu.VMEM(block_scales.shape[::-1], jnp.float32),
            pltpu.VMEM(factor_down.shape, jnp.float32),
            pltpu.VMEM(factor_up.shape, jnp.float32),
            pltpu.VMEM(moment_down.shape, jnp.float32),
            pltpu.VMEM(second_down.shape, jnp.float32),
            pltpu.VMEM(moment_up.shape, jnp.float32),
            pltpu.VMEM(second_up.shape, jnp.float32),
            dma((13,)),
            pltpu.VMEM((fsdp, rank, width + value), low),
            pltpu.VMEM((2, planes, rank, width + value), low),
            pltpu.VMEM((planes, rank, width + value), low),
            pltpu.VMEM((planes, rank, width + value), low),
            pltpu.VMEM((planes, rank, width + value), low),
            pltpu.VMEM((tensor, 2, 2, tok_rows, value), low),
            pltpu.VMEM((tensor, 2 * rank, tok_rows), jnp.float32),
            pltpu.VMEM((wide, 2, CHUNKS, step_rows, value), low),
            pltpu.VMEM((tensor, CHUNKS, step_rows, value), low),
            pltpu.VMEM((CHUNKS, 2, 2, tok_rows, step_rows), low),
            pltpu.VMEM((2, 2, CHUNKS, tok_rows, step_rows), low),
            pltpu.VMEM((tok_rows, width), jnp.float32),
            dma((planes,)),
            dma((planes,)),
            dma((fsdp,)),
            dma((1,)),
            dma((1,)),
            dma((planes,)),
            dma((planes,)),
            dma((1,)),
            dma((2,)),
            dma((4, wide)),
            dma((4, wide)),
            dma((tensor, 2, 2)),
            dma((tensor,)),
            dma((tensor,)),
            dma((wide, 2, CHUNKS)),
            dma((wide, 2, CHUNKS)),
            dma((wide, 2, CHUNKS)),
            dma((tensor, CHUNKS)),
            dma((CHUNKS, 2, 2)),
            dma((2, 2, CHUNKS)),
        ],
        compiler_params=pltpu.CompilerParams(
            collective_id=0, has_side_effects=True, vmem_limit_bytes=60 * 1024 * 1024
        ),
    )(
        tenant_ids,
        live_counts,
        tenant_owner,
        layer_input,
        value_grad,
        quant_codes,
        block_scales.T,
        factor_down,
        factor_up,
        moment_down,
        second_down,
        moment_up,
        second_up,
    )
    return pl.pallas_call(
        functools.partial(write_kernel, len(shapes)),
        out_shape=shapes,
        in_specs=[anywhere] * len(shapes),
        out_specs=(anywhere,) * len(shapes),
        scratch_shapes=[pltpu.VMEM(s.shape, s.dtype) for s in shapes] + [dma((2, len(shapes)))],
        compiler_params=pltpu.CompilerParams(vmem_limit_bytes=60 * 1024 * 1024),
    )(*results)


def solution(mesh):
    fsdp, tensor = mesh.shape["fsdp"], mesh.shape["tensor"]
    planar = fsdp == 2 * tensor and tensor % 2 == 0
    body = functools.partial(fused, fsdp, tensor) if planar else shards
    in_specs = (
        P("fsdp", "tensor"),
        P("fsdp", "tensor"),
        P("fsdp", "tensor"),
        P("fsdp", "tensor"),
        P("fsdp"),
        P("fsdp"),
        P(),
        P("fsdp", None, "tensor"),
        P("fsdp", None, "tensor"),
        P("fsdp", None, "tensor"),
        P("fsdp", None, "tensor"),
        P("fsdp", None, "tensor"),
        P("fsdp", None, "tensor"),
    )
    out_specs = (
        P("fsdp", "tensor"),
        P("fsdp", None, "tensor"),
        P("fsdp", None, "tensor"),
        P("fsdp", None, "tensor"),
        P("fsdp", None, "tensor"),
        P("fsdp", None, "tensor"),
        P("fsdp", None, "tensor"),
    )
    return jax.shard_map(body, mesh=mesh, in_specs=in_specs, out_specs=out_specs, check_vma=False)
```

```python
import functools
import math

import jax
import jax.numpy as jnp
from jax import lax
from jax.experimental import pallas as pl
from jax.experimental.pallas import tpu as pltpu
from jax.sharding import PartitionSpec as P

MODEL_WIDTH = 8192
ADAPTER_RANK = 16


nf4_levels = (
    -1.0,
    -0.6962,
    -0.5251,
    -0.3949,
    -0.2844,
    -0.1848,
    -0.0911,
    0.0,
    0.0796,
    0.1609,
    0.2461,
    0.3379,
    0.4407,
    0.5626,
    0.723,
    1.0,
)
adapter_scale = 2.0
beta_one = 0.9
beta_two = 0.999
adam_step = 10.0
learn_rate = 0.05
decay_rate = 0.01
adam_eps = 1e-08


def adam_update(param, grad, moment, second):
    new_moment = beta_one * moment + (1.0 - beta_one) * grad
    new_second = beta_two * second + (1.0 - beta_two) * grad * grad
    corrected = new_moment / (1.0 - beta_one**adam_step)
    divisor = jnp.sqrt(new_second / (1.0 - beta_two**adam_step)) + adam_eps
    new_param = param - learn_rate * (corrected / divisor + decay_rate * param)
    return (new_param, new_moment, new_second)


def dequantize(quant_codes, block_scales):
    levels_out = jnp.zeros(quant_codes.shape, jnp.float32)
    for position in range(16):
        levels_out = jnp.where(quant_codes == position, nf4_levels[position], levels_out)
    row_count, col_count = quant_codes.shape
    blocks = block_scales.shape[1]
    scaled = levels_out.reshape(row_count, blocks, col_count // blocks) * block_scales[:, :, None]
    return scaled.reshape(row_count, col_count).astype(jnp.bfloat16)


def right_product(left, right):
    return lax.dot_general(
        left, right, (((1,), (1,)), ((), ())), preferred_element_type=jnp.float32
    )


def left_product(left, right):
    return lax.dot_general(
        left, right, (((0,), (0,)), ((), ())), preferred_element_type=jnp.float32
    )


def add_sources(pieces):
    return (jnp.sum(pieces[0], axis=0, keepdims=True), jnp.sum(pieces[1], axis=0, keepdims=True))


def shards(
    layer_input,
    value_grad,
    quant_codes,
    block_scales,
    tenant_ids,
    live_counts,
    tenant_owner,
    factor_down,
    factor_up,
    moment_down,
    second_down,
    moment_up,
    second_up,
):
    tok_rows, width_part = layer_input.shape
    value_part = value_grad.shape[1]
    slot_count = tenant_ids.shape[0]
    seq_len = tok_rows // slot_count
    tenant_total = tenant_owner.shape[0]
    rank_size = factor_down.shape[1]
    inverse_width = 1.0 / math.sqrt(MODEL_WIDTH)
    coefficient = adapter_scale / math.sqrt(ADAPTER_RANK)
    live_seq = jnp.arange(slot_count, dtype=jnp.int32) < live_counts[0]
    live_tok = jnp.broadcast_to(live_seq[:, None], (slot_count, seq_len)).reshape(tok_rows)
    masked = jnp.where(live_tok[:, None], value_grad, jnp.zeros_like(value_grad))
    tenant_iota = jnp.arange(tenant_total, dtype=jnp.int32)
    matches = tenant_ids[:, None] == tenant_iota[None, :]
    slot_seq = jnp.sum(jnp.where(matches, tenant_owner[None, :], 0), axis=1)
    onehot_seq = (slot_seq[:, None] == tenant_iota[None, :]).astype(jnp.bfloat16)
    weight_local = dequantize(quant_codes, block_scales)
    all_down, all_up = (
        lax.all_gather(factor_down.astype(jnp.bfloat16), "fsdp", axis=0, tiled=True),
        lax.all_gather(factor_up.astype(jnp.bfloat16), "fsdp", axis=0, tiled=True),
    )
    partial_value = right_product(masked, lax.all_gather(weight_local, "fsdp", axis=0, tiled=True))
    base_input_grad = lax.psum_scatter(
        partial_value.astype(jnp.bfloat16), "tensor", scatter_dimension=1, tiled=True
    ).astype(jnp.float32)
    flattened_down = all_down.reshape(tenant_total * rank_size, width_part)
    up_flat = all_up.reshape(tenant_total * rank_size, value_part)
    onehot_tok = jnp.broadcast_to(
        onehot_seq[:, None, :], (slot_count, seq_len, tenant_total)
    ).reshape(tok_rows, tenant_total)
    selector = onehot_tok.astype(jnp.float32)[:, :, None]
    down_scores = right_product(layer_input, flattened_down).reshape(
        tok_rows, tenant_total, rank_size
    )
    up_scores = right_product(masked, up_flat).reshape(tok_rows, tenant_total, rank_size)
    in_part = jnp.sum(down_scores * selector, axis=1) * inverse_width
    grad_part = jnp.sum(up_scores * selector, axis=1) * coefficient
    in_sum, grad_sum = lax.psum((in_part, grad_part), "tensor")
    input_lowrank = in_sum.astype(jnp.bfloat16)
    gradient_lowrank = grad_sum.astype(jnp.bfloat16)
    spread_gradient = (onehot_tok[:, :, None] * gradient_lowrank[:, None, :]).reshape(
        tok_rows, tenant_total * rank_size
    )
    in_spread = (onehot_tok[:, :, None] * input_lowrank[:, None, :]).reshape(
        tok_rows, tenant_total * rank_size
    )
    adapter_input_grad = (
        jnp.dot(spread_gradient, flattened_down, preferred_element_type=jnp.float32) * inverse_width
    )
    down_terms = (left_product(spread_gradient, layer_input) * inverse_width).reshape(
        tenant_total, rank_size, width_part
    )
    up_terms = (left_product(in_spread, masked) * coefficient).reshape(
        tenant_total, rank_size, value_part
    )
    down_gradient, up_gradient = add_sources(
        (
            lax.all_to_all(
                down_terms.astype(jnp.bfloat16), "fsdp", split_axis=0, concat_axis=0, tiled=True
            ).astype(down_terms.dtype),
            lax.all_to_all(
                up_terms.astype(jnp.bfloat16), "fsdp", split_axis=0, concat_axis=0, tiled=True
            ).astype(up_terms.dtype),
        )
    )
    layer_input_gradient = (base_input_grad + adapter_input_grad).astype(jnp.bfloat16)
    new_down, new_moment_down, new_second_down = adam_update(
        factor_down, down_gradient, moment_down, second_down
    )
    new_up, new_moment_up, new_second_up = adam_update(factor_up, up_gradient, moment_up, second_up)
    return (
        layer_input_gradient,
        new_down,
        new_up,
        new_moment_down,
        new_second_down,
        new_moment_up,
        new_second_up,
    )


CHUNKS = 4


def level_tree(codes):
    rows = [jnp.float32(level) for level in nf4_levels]
    for bit in range(4):
        chosen = (codes & (1 << bit)) != 0
        rows = [jnp.where(chosen, rows[2 * n + 1], rows[2 * n]) for n in range(len(rows) // 2)]
    return rows[0]


def fused_kernel(
    fsdp,
    tensor,
    ids_any,
    live_any,
    owner_any,
    x_any,
    dv_any,
    code_any,
    scale_any,
    fd_any,
    fu_any,
    md_any,
    sd_any,
    mu_any,
    su_any,
    out_ref,
    nd_ref,
    nu_ref,
    nmd_ref,
    nsd_ref,
    nmu_ref,
    nsu_ref,
    ids_ref,
    live_ref,
    owner_ref,
    x_ref,
    dv_ref,
    code_ref,
    scale_ref,
    fd_ref,
    fu_ref,
    md_ref,
    sd_ref,
    mu_ref,
    su_ref,
    in_s,
    fac,
    gsend,
    gy,
    gz,
    grecv,
    dvs,
    part,
    col,
    wgt,
    outs,
    base,
    lows,
    fac_s,
    fac_f,
    fac_r,
    gy_s,
    gy_r,
    gz_s,
    gz_r,
    dvz_s,
    dvy_s,
    dvx_s,
    dvc_s,
    dv_r,
    part_s,
    part_r,
    col_s,
    col_r,
    wgt_s,
    wgt_r,
    out_s,
    out_r,
):
    f = lax.axis_index("fsdp")
    t = lax.axis_index("tensor")
    z, y = f // 2, f % 2
    x, c = t // 2, t % 2
    pair, odd = z // 2, z % 2
    wide, planes = tensor // 2, fsdp // 2
    tok_rows, width = x_ref.shape
    value = dv_ref.shape[1]
    w_rows = code_ref.shape[0]
    step_rows = w_rows // (2 * CHUNKS)
    rank = fd_ref.shape[1]
    slots = ids_ref.shape[0]
    seq = tok_rows // slots
    flat = fsdp * rank
    inverse_width = 1.0 / math.sqrt(MODEL_WIDTH)
    coefficient = adapter_scale / math.sqrt(ADAPTER_RANK)
    pending = []

    loads = {}
    for n, (name, src, dst) in enumerate(
        (
            ("fd", fd_any, fd_ref),
            ("fu", fu_any, fu_ref),
            ("dv", dv_any, dv_ref),
            ("live", live_any, live_ref),
            ("scale", scale_any, scale_ref),
            ("code", code_any, code_ref),
            ("x", x_any, x_ref),
            ("ids", ids_any, ids_ref),
            ("owner", owner_any, owner_ref),
            ("md", md_any, md_ref),
            ("sd", sd_any, sd_ref),
            ("mu", mu_any, mu_ref),
            ("su", su_any, su_ref),
        )
    ):
        loads[name] = pltpu.make_async_copy(src, dst, in_s.at[n])
        loads[name].start()

    def remote(src, dst, ss, rs, df, dt):
        return pltpu.make_async_remote_copy(
            src_ref=src,
            dst_ref=dst,
            send_sem=ss,
            recv_sem=rs,
            device_id={"fsdp": df, "tensor": dt},
            device_id_type=pl.DeviceIdType.MESH,
        )

    def send(copy, cond=None):
        if cond is None:
            copy.start()
        else:
            pl.when(cond)(copy.start)
        pending.append((copy, cond))

    barrier = pltpu.get_barrier_semaphore()
    greeted = []

    def greet(df, dt):
        pl.semaphore_signal(
            barrier,
            inc=1,
            device_id={"fsdp": df, "tensor": dt},
            device_id_type=pl.DeviceIdType.MESH,
        )
        greeted.append(1)

    for n in range(1, 8):
        near = 2 * pair + (odd + n // 4) % 2
        greet(2 * near + (y + n // 2) % 2, 2 * x + (c + n) % 2)
    for d in range(1, wide):
        for e in range(2):
            greet(2 * (2 * ((pair + d) % wide) + e) + y, t)
            greet(f, 2 * ((x + d) % wide) + e)

    loads["fd"].wait()
    loads["fu"].wait()
    fac[pl.ds(f, 1), :, 0:width] = fd_ref[...].astype(jnp.bfloat16)
    fac[pl.ds(f, 1), :, width : width + value] = fu_ref[...].astype(jnp.bfloat16)
    loads["dv"].wait()
    loads["live"].wait()
    tok_index = lax.broadcasted_iota(jnp.int32, (tok_rows, value), 0)
    masked = jnp.where(
        tok_index < live_ref[0] * seq, dv_ref[...].astype(jnp.float32), 0.0
    ).astype(jnp.bfloat16)
    dvs[t, odd, y] = masked

    def dequant(half, chunk):
        rows = pl.ds((half * CHUNKS + chunk) * step_rows, step_rows)
        levels = level_tree(code_ref[rows, :])
        scales = jnp.transpose(scale_ref[:, rows])
        blocks = scales.shape[1]
        block = value // blocks
        lane = lax.broadcasted_iota(jnp.int32, (step_rows, value), 1)
        spread = jnp.broadcast_to(scales[:, blocks - 1 : blocks], (step_rows, value))
        for n in reversed(range(blocks - 1)):
            spread = jnp.where(lane < (n + 1) * block, scales[:, n : n + 1], spread)
        col[pair, half, chunk] = (levels * spread).astype(jnp.bfloat16)

    loads["scale"].wait()
    loads["code"].wait()
    dequant(0, 0)
    dequant(1, 0)
    pl.semaphore_wait(barrier, len(greeted))

    def fac_copy(dz, source):
        return remote(
            fac.at[source], fac.at[source], fac_s.at[dz], fac_r.at[source], (f + 2 * dz) % fsdp, t
        )

    def fac_forward(dz, source):
        return remote(
            fac.at[source], fac.at[source], fac_f.at[dz], fac_r.at[source], 2 * z + 1 - y, t
        )

    for dz in range(1, planes):
        send(fac_copy(dz, f))
    send(fac_forward(0, f))

    def dv_near(parity, sy):
        ref = dvs.at[t, parity, sy]
        return remote(ref, ref, dvz_s.at[0], dv_r.at[t, parity, sy], 2 * (4 * pair + 1 - z) + y, t)

    def dv_over(n, parity, sy):
        ref = dvs.at[t, parity, sy]
        return remote(ref, ref, dvy_s.at[n], dv_r.at[t, parity, sy], 2 * z + 1 - y, t)

    def dv_along(n, d, st, parity, sy):
        ref = dvs.at[st, parity, sy]
        to = 2 * ((x + d) % wide) + c
        return remote(ref, ref, dvx_s.at[n, d], dv_r.at[st, parity, sy], f, to)

    def dv_core(n, d, st, parity, sy):
        ref = dvs.at[st, parity, sy]
        return remote(ref, ref, dvc_s.at[n, d], dv_r.at[st, parity, sy], f, 2 * x + 1 - c)

    def dv_share(n, parity, sy):
        for d in range(1, wide):
            send(dv_along(n, d, t, parity, sy))
        send(dv_core(n, 0, t, parity, sy))

    send(dv_near(odd, y))
    send(dv_over(0, odd, y))
    dv_share(0, odd, y)

    def col_copy(d, source, half, chunk):
        ref = col.at[source, half, chunk]
        return remote(
            ref,
            ref,
            col_s.at[d, half, chunk],
            col_r.at[source, half, chunk],
            2 * (2 * ((pair + d) % wide) + odd) + y,
            t,
        )

    def wgt_copy(d, source, half, chunk):
        return remote(
            col.at[source, half, chunk],
            wgt.at[t, chunk],
            wgt_s.at[d, half, chunk],
            wgt_r.at[t, chunk],
            f,
            2 * source + half,
        )

    def hand_out(d, half, chunk):
        source = (pair + d) % wide
        send(wgt_copy(d, source, half, chunk), 2 * source + half != t)

    for chunk in range(CHUNKS):
        for half in range(2):
            if chunk > 0:
                dequant(half, chunk)
            for d in range(1, wide):
                send(col_copy(d, pair, half, chunk))

    def forward(chunk):
        for d in range(1, wide):
            for half in range(2):
                col_copy(d, (pair + d) % wide, half, chunk).wait_recv()
                hand_out(d, half, chunk)

    def give(chunk):
        for half in range(2):
            hand_out(0, half, chunk)

    give(0)
    dv_over(0, odd, 1 - y).wait_recv()
    dv_share(1, odd, 1 - y)
    for dz in range(1, planes):
        source = (f + 2 * dz) % fsdp
        fac_copy(dz, source).wait_recv()
        send(fac_forward(dz, source))
    dv_near(1 - odd, y).wait_recv()
    send(dv_over(1, 1 - odd, y))
    dv_share(2, 1 - odd, y)
    give(1)
    dv_over(1, 1 - odd, 1 - y).wait_recv()
    dv_share(3, 1 - odd, 1 - y)
    for later in range(2, CHUNKS):
        give(later)

    loads["ids"].wait()
    loads["owner"].wait()
    slot_row = jnp.zeros((1, tok_rows), jnp.int32)
    seq_row = lax.broadcasted_iota(jnp.int32, (1, tok_rows), 1) // seq
    for n in range(slots):
        own = jnp.int32(0)
        for u in range(fsdp):
            own = own + jnp.where(ids_ref[n] == u, owner_ref[u], 0)
        slot_row = jnp.where(seq_row == n, own, slot_row)
    named = lax.broadcasted_iota(jnp.int32, (flat, tok_rows), 0) // rank
    chosen = named == jnp.broadcast_to(slot_row, (flat, tok_rows))

    forward(0)
    for dz in range(planes):
        source = (2 * z + 2 * dz) % fsdp + 1 - y
        fac_forward(dz, source).wait_recv()
    loads["x"].wait()
    all_down = fac[:, :, 0:width].reshape(flat, width)
    all_up = fac[:, :, width : width + value].reshape(flat, value)

    def folded(scores, factor):
        kept = jnp.where(chosen, scores, 0.0).reshape(fsdp, rank, tok_rows)
        return jnp.sum(kept, axis=0) * factor

    part[t, 0:rank, :] = folded(right_product(all_down, x_ref[...]), inverse_width)
    part[t, rank : 2 * rank, :] = folded(right_product(all_up, masked), coefficient)

    def part_copy(dt, source):
        return remote(part.at[source], part.at[source], part_s.at[dt], part_r.at[source], f, dt)

    for step in range(1, tensor):
        send(part_copy((t + step) % tensor, t))

    for n, (parity, sy) in enumerate(
        ((odd, y), (odd, 1 - y), (1 - odd, y), (1 - odd, 1 - y))
    ):
        for d in range(1, wide):
            st = 2 * ((x + d) % wide) + c
            dv_along(n, d, st, parity, sy).wait_recv()
            send(dv_core(n, d, st, parity, sy))
    forward(1)

    for step in range(1, tensor):
        source = (t + step) % tensor
        part_copy(source, source).wait_recv()
    sums = jnp.sum(part[...], axis=0)
    low = sums.astype(jnp.bfloat16).astype(jnp.float32)

    def spread_out(rows):
        tiled = jnp.broadcast_to(rows[None], (fsdp, rank, tok_rows)).reshape(flat, tok_rows)
        return jnp.where(chosen, tiled, 0.0).astype(jnp.bfloat16)

    in_spread = spread_out(low[0:rank])
    grad_spread = spread_out(low[rank : 2 * rank])
    down_terms = jnp.dot(grad_spread, x_ref[...], preferred_element_type=jnp.float32)
    by_slot = (down_terms * inverse_width).astype(jnp.bfloat16).reshape(fsdp, rank, width)
    up_terms = jnp.dot(in_spread, masked, preferred_element_type=jnp.float32)
    up_slot = (up_terms * coefficient).astype(jnp.bfloat16).reshape(fsdp, rank, value)
    for slot in range(fsdp):
        gsend[slot % 2, slot // 2, :, 0:width] = by_slot[slot]
        gsend[slot % 2, slot // 2, :, width : width + value] = up_slot[slot]
    over = remote(gsend.at[1 - y], gy, gy_s.at[0], gy_r.at[0], 2 * z + 1 - y, t)
    send(over)

    def grad_copy(dz, to, source):
        return remote(
            gz.at[to], grecv.at[source], gz_s.at[dz], gz_r.at[source], (f + 2 * dz) % fsdp, t
        )

    for d in range(wide):
        for parity in range(2):
            for sy in range(2):
                dv_core(0, 0, 2 * d + 1 - c, parity, sy).wait_recv()

    def multiply(chunk):
        for step in range(1, tensor):
            source = (t + step) % tensor
            arrived = remote(
                col.at[0, 0, chunk],
                wgt.at[source, chunk],
                wgt_s.at[0, 0, chunk],
                wgt_r.at[source, chunk],
                f,
                source,
            )
            arrived.wait_recv()
        rows = 4 * tok_rows
        total = right_product(dvs[t].reshape(rows, value), col[x, c, chunk])
        for step in range(1, tensor):
            source = (t + step) % tensor
            total = total + right_product(dvs[source].reshape(rows, value), wgt[source, chunk])
        for parity in range(2):
            for half in range(2):
                start = (2 * parity + half) * tok_rows
                piece = total[start : start + tok_rows].astype(jnp.bfloat16)
                outs[chunk, parity, half] = piece
                df, dt = 2 * (2 * pair + parity) + half, 2 * x + odd
                stays = jnp.logical_and(df == f, dt == t)

                @pl.when(stays)
                def _(piece=piece):
                    base[y, c, chunk] = piece

                copy = remote(
                    outs.at[chunk, parity, half],
                    base.at[y, c, chunk],
                    out_s.at[chunk, parity, half],
                    out_r.at[y, c, chunk],
                    df,
                    dt,
                )
                send(copy, jnp.logical_not(stays))

    multiply(0)
    over.wait_recv()
    gz[...] = (gsend[y].astype(jnp.float32) + gy[...].astype(jnp.float32)).astype(jnp.bfloat16)
    for dz in range(1, planes):
        send(grad_copy(dz, (z + dz) % planes, z))
    grecv[pl.ds(z, 1)] = gz[pl.ds(z, 1)]
    multiply(1)
    forward(2)
    multiply(2)
    lows[...] = inverse_width * lax.dot_general(
        grad_spread, all_down, (((0,), (0,)), ((), ())), preferred_element_type=jnp.float32
    )
    for later in range(3, CHUNKS):
        forward(later)
        multiply(later)

    def finish(chunk):
        for half in range(2):
            for core in range(2):
                stays = jnp.logical_and(odd == c, jnp.logical_and(half == y, core == c))
                arrived = remote(
                    outs.at[chunk, 0, 0],
                    base.at[half, core, chunk],
                    out_s.at[chunk, 0, 0],
                    out_r.at[half, core, chunk],
                    f,
                    2 * x + 1 - c,
                )
                pl.when(jnp.logical_not(stays))(arrived.wait_recv)
                start = half * w_rows + (core * CHUNKS + chunk) * step_rows
                stop = start + step_rows
                out_ref[:, start:stop] = (
                    base[half, core, chunk].astype(jnp.float32) + lows[:, start:stop]
                ).astype(jnp.bfloat16)

    for chunk in range(CHUNKS - 1):
        finish(chunk)
    for dz in range(1, planes):
        grad_copy(dz, 0, (z + dz) % planes).wait_recv()
    for name in ("md", "sd", "mu", "su"):
        loads[name].wait()
    down_grad = jnp.sum(grecv[:, :, 0:width].astype(jnp.float32), axis=0, keepdims=True)
    up_grad = jnp.sum(
        grecv[:, :, width : width + value].astype(jnp.float32), axis=0, keepdims=True
    )
    nd_ref[...], nmd_ref[...], nsd_ref[...] = adam_update(
        fd_ref[...], down_grad, md_ref[...], sd_ref[...]
    )
    nu_ref[...], nmu_ref[...], nsu_ref[...] = adam_update(
        fu_ref[...], up_grad, mu_ref[...], su_ref[...]
    )

    finish(CHUNKS - 1)

    for copy, cond in pending:
        if cond is None:
            copy.wait_send()
        else:
            pl.when(cond)(copy.wait_send)


def write_kernel(count, *refs):
    held, sems = refs[2 * count : 3 * count], refs[3 * count]
    loads = [pltpu.make_async_copy(refs[n], held[n], sems.at[0, n]) for n in range(count)]
    stores = [pltpu.make_async_copy(held[n], refs[count + n], sems.at[1, n]) for n in range(count)]
    for load in loads:
        load.start()
    for load, store in zip(loads, stores):
        load.wait()
        store.start()
    for store in stores:
        store.wait()


def fused(fsdp, tensor, *args):
    (
        layer_input,
        value_grad,
        quant_codes,
        block_scales,
        tenant_ids,
        live_counts,
        tenant_owner,
        factor_down,
        factor_up,
        moment_down,
        second_down,
        moment_up,
        second_up,
    ) = args
    tok_rows, width = layer_input.shape
    value = value_grad.shape[1]
    w_rows = quant_codes.shape[0]
    rank = factor_down.shape[1]
    step_rows = w_rows // (2 * CHUNKS)
    wide, planes = tensor // 2, fsdp // 2
    low = jnp.bfloat16
    dma = pltpu.SemaphoreType.DMA
    vmem = pl.BlockSpec(memory_space=pltpu.VMEM)
    like = jax.ShapeDtypeStruct
    shapes = (
        like(layer_input.shape, low),
        like(factor_down.shape, jnp.float32),
        like(factor_up.shape, jnp.float32),
        like(factor_down.shape, jnp.float32),
        like(factor_down.shape, jnp.float32),
        like(factor_up.shape, jnp.float32),
        like(factor_up.shape, jnp.float32),
    )
    anywhere = pl.BlockSpec(memory_space=pl.ANY)
    results = pl.pallas_call(
        functools.partial(fused_kernel, fsdp, tensor),
        out_shape=shapes,
        in_specs=[anywhere] * 13,
        out_specs=(vmem,) * 7,
        scratch_shapes=[
            pltpu.SMEM(tenant_ids.shape, jnp.int32),
            pltpu.SMEM(live_counts.shape, jnp.int32),
            pltpu.SMEM(tenant_owner.shape, jnp.int32),
            pltpu.VMEM(layer_input.shape, low),
            pltpu.VMEM(value_grad.shape, low),
            pltpu.VMEM(quant_codes.shape, jnp.int32),
            pltpu.VMEM(block_scales.shape[::-1], jnp.float32),
            pltpu.VMEM(factor_down.shape, jnp.float32),
            pltpu.VMEM(factor_up.shape, jnp.float32),
            pltpu.VMEM(moment_down.shape, jnp.float32),
            pltpu.VMEM(second_down.shape, jnp.float32),
            pltpu.VMEM(moment_up.shape, jnp.float32),
            pltpu.VMEM(second_up.shape, jnp.float32),
            dma((13,)),
            pltpu.VMEM((fsdp, rank, width + value), low),
            pltpu.VMEM((2, planes, rank, width + value), low),
            pltpu.VMEM((planes, rank, width + value), low),
            pltpu.VMEM((planes, rank, width + value), low),
            pltpu.VMEM((planes, rank, width + value), low),
            pltpu.VMEM((tensor, 2, 2, tok_rows, value), low),
            pltpu.VMEM((tensor, 2 * rank, tok_rows), jnp.float32),
            pltpu.VMEM((wide, 2, CHUNKS, step_rows, value), low),
            pltpu.VMEM((tensor, CHUNKS, step_rows, value), low),
            pltpu.VMEM((CHUNKS, 2, 2, tok_rows, step_rows), low),
            pltpu.VMEM((2, 2, CHUNKS, tok_rows, step_rows), low),
            pltpu.VMEM((tok_rows, width), jnp.float32),
            dma((planes,)),
            dma((planes,)),
            dma((fsdp,)),
            dma((1,)),
            dma((1,)),
            dma((planes,)),
            dma((planes,)),
            dma((1,)),
            dma((2,)),
            dma((4, wide)),
            dma((4, wide)),
            dma((tensor, 2, 2)),
            dma((tensor,)),
            dma((tensor,)),
            dma((wide, 2, CHUNKS)),
            dma((wide, 2, CHUNKS)),
            dma((wide, 2, CHUNKS)),
            dma((tensor, CHUNKS)),
            dma((CHUNKS, 2, 2)),
            dma((2, 2, CHUNKS)),
        ],
        compiler_params=pltpu.CompilerParams(
            collective_id=0, has_side_effects=True, vmem_limit_bytes=60 * 1024 * 1024
        ),
    )(
        tenant_ids,
        live_counts,
        tenant_owner,
        layer_input,
        value_grad,
        quant_codes,
        block_scales.T,
        factor_down,
        factor_up,
        moment_down,
        second_down,
        moment_up,
        second_up,
    )
    return pl.pallas_call(
        functools.partial(write_kernel, len(shapes)),
        out_shape=shapes,
        in_specs=[anywhere] * len(shapes),
        out_specs=(anywhere,) * len(shapes),
        scratch_shapes=[pltpu.VMEM(s.shape, s.dtype) for s in shapes] + [dma((2, len(shapes)))],
        compiler_params=pltpu.CompilerParams(vmem_limit_bytes=60 * 1024 * 1024),
    )(*results)


def solution(mesh):
    fsdp, tensor = mesh.shape["fsdp"], mesh.shape["tensor"]
    planar = fsdp == 2 * tensor and tensor % 2 == 0
    body = functools.partial(fused, fsdp, tensor) if planar else shards
    in_specs = (
        P("fsdp", "tensor"),
        P("fsdp", "tensor"),
        P("fsdp", "tensor"),
        P("fsdp", "tensor"),
        P("fsdp"),
        P("fsdp"),
        P(),
        P("fsdp", None, "tensor"),
        P("fsdp", None, "tensor"),
        P("fsdp", None, "tensor"),
        P("fsdp", None, "tensor"),
        P("fsdp", None, "tensor"),
        P("fsdp", None, "tensor"),
    )
    out_specs = (
        P("fsdp", "tensor"),
        P("fsdp", None, "tensor"),
        P("fsdp", None, "tensor"),
        P("fsdp", None, "tensor"),
        P("fsdp", None, "tensor"),
        P("fsdp", None, "tensor"),
        P("fsdp", None, "tensor"),
    )
    return jax.shard_map(body, mesh=mesh, in_specs=in_specs, out_specs=out_specs, check_vma=False)
```

```python
import functools
import math

import jax
import jax.numpy as jnp
from jax import lax
from jax.experimental import pallas as pl
from jax.experimental.pallas import tpu as pltpu
from jax.sharding import PartitionSpec as P

MODEL_WIDTH = 8192
ADAPTER_RANK = 16


nf4_levels = (
    -1.0,
    -0.6962,
    -0.5251,
    -0.3949,
    -0.2844,
    -0.1848,
    -0.0911,
    0.0,
    0.0796,
    0.1609,
    0.2461,
    0.3379,
    0.4407,
    0.5626,
    0.723,
    1.0,
)
adapter_scale = 2.0
beta_one = 0.9
beta_two = 0.999
adam_step = 10.0
learn_rate = 0.05
decay_rate = 0.01
adam_eps = 1e-08


def adam_update(param, grad, moment, second):
    new_moment = beta_one * moment + (1.0 - beta_one) * grad
    new_second = beta_two * second + (1.0 - beta_two) * grad * grad
    corrected = new_moment / (1.0 - beta_one**adam_step)
    divisor = jnp.sqrt(new_second / (1.0 - beta_two**adam_step)) + adam_eps
    new_param = param - learn_rate * (corrected / divisor + decay_rate * param)
    return (new_param, new_moment, new_second)


def dequantize(quant_codes, block_scales):
    levels_out = jnp.zeros(quant_codes.shape, jnp.float32)
    for position in range(16):
        levels_out = jnp.where(quant_codes == position, nf4_levels[position], levels_out)
    row_count, col_count = quant_codes.shape
    blocks = block_scales.shape[1]
    scaled = levels_out.reshape(row_count, blocks, col_count // blocks) * block_scales[:, :, None]
    return scaled.reshape(row_count, col_count).astype(jnp.bfloat16)


def right_product(left, right):
    return lax.dot_general(
        left, right, (((1,), (1,)), ((), ())), preferred_element_type=jnp.float32
    )


def left_product(left, right):
    return lax.dot_general(
        left, right, (((0,), (0,)), ((), ())), preferred_element_type=jnp.float32
    )


def add_sources(pieces):
    return (jnp.sum(pieces[0], axis=0, keepdims=True), jnp.sum(pieces[1], axis=0, keepdims=True))


def shards(
    layer_input,
    value_grad,
    quant_codes,
    block_scales,
    tenant_ids,
    live_counts,
    tenant_owner,
    factor_down,
    factor_up,
    moment_down,
    second_down,
    moment_up,
    second_up,
):
    tok_rows, width_part = layer_input.shape
    value_part = value_grad.shape[1]
    slot_count = tenant_ids.shape[0]
    seq_len = tok_rows // slot_count
    tenant_total = tenant_owner.shape[0]
    rank_size = factor_down.shape[1]
    inverse_width = 1.0 / math.sqrt(MODEL_WIDTH)
    coefficient = adapter_scale / math.sqrt(ADAPTER_RANK)
    live_seq = jnp.arange(slot_count, dtype=jnp.int32) < live_counts[0]
    live_tok = jnp.broadcast_to(live_seq[:, None], (slot_count, seq_len)).reshape(tok_rows)
    masked = jnp.where(live_tok[:, None], value_grad, jnp.zeros_like(value_grad))
    tenant_iota = jnp.arange(tenant_total, dtype=jnp.int32)
    matches = tenant_ids[:, None] == tenant_iota[None, :]
    slot_seq = jnp.sum(jnp.where(matches, tenant_owner[None, :], 0), axis=1)
    onehot_seq = (slot_seq[:, None] == tenant_iota[None, :]).astype(jnp.bfloat16)
    weight_local = dequantize(quant_codes, block_scales)
    all_down, all_up = (
        lax.all_gather(factor_down.astype(jnp.bfloat16), "fsdp", axis=0, tiled=True),
        lax.all_gather(factor_up.astype(jnp.bfloat16), "fsdp", axis=0, tiled=True),
    )
    partial_value = right_product(masked, lax.all_gather(weight_local, "fsdp", axis=0, tiled=True))
    base_input_grad = lax.psum_scatter(
        partial_value.astype(jnp.bfloat16), "tensor", scatter_dimension=1, tiled=True
    ).astype(jnp.float32)
    flattened_down = all_down.reshape(tenant_total * rank_size, width_part)
    up_flat = all_up.reshape(tenant_total * rank_size, value_part)
    onehot_tok = jnp.broadcast_to(
        onehot_seq[:, None, :], (slot_count, seq_len, tenant_total)
    ).reshape(tok_rows, tenant_total)
    selector = onehot_tok.astype(jnp.float32)[:, :, None]
    down_scores = right_product(layer_input, flattened_down).reshape(
        tok_rows, tenant_total, rank_size
    )
    up_scores = right_product(masked, up_flat).reshape(tok_rows, tenant_total, rank_size)
    in_part = jnp.sum(down_scores * selector, axis=1) * inverse_width
    grad_part = jnp.sum(up_scores * selector, axis=1) * coefficient
    in_sum, grad_sum = lax.psum((in_part, grad_part), "tensor")
    input_lowrank = in_sum.astype(jnp.bfloat16)
    gradient_lowrank = grad_sum.astype(jnp.bfloat16)
    spread_gradient = (onehot_tok[:, :, None] * gradient_lowrank[:, None, :]).reshape(
        tok_rows, tenant_total * rank_size
    )
    in_spread = (onehot_tok[:, :, None] * input_lowrank[:, None, :]).reshape(
        tok_rows, tenant_total * rank_size
    )
    adapter_input_grad = (
        jnp.dot(spread_gradient, flattened_down, preferred_element_type=jnp.float32) * inverse_width
    )
    down_terms = (left_product(spread_gradient, layer_input) * inverse_width).reshape(
        tenant_total, rank_size, width_part
    )
    up_terms = (left_product(in_spread, masked) * coefficient).reshape(
        tenant_total, rank_size, value_part
    )
    down_gradient, up_gradient = add_sources(
        (
            lax.all_to_all(
                down_terms.astype(jnp.bfloat16), "fsdp", split_axis=0, concat_axis=0, tiled=True
            ).astype(down_terms.dtype),
            lax.all_to_all(
                up_terms.astype(jnp.bfloat16), "fsdp", split_axis=0, concat_axis=0, tiled=True
            ).astype(up_terms.dtype),
        )
    )
    layer_input_gradient = (base_input_grad + adapter_input_grad).astype(jnp.bfloat16)
    new_down, new_moment_down, new_second_down = adam_update(
        factor_down, down_gradient, moment_down, second_down
    )
    new_up, new_moment_up, new_second_up = adam_update(factor_up, up_gradient, moment_up, second_up)
    return (
        layer_input_gradient,
        new_down,
        new_up,
        new_moment_down,
        new_second_down,
        new_moment_up,
        new_second_up,
    )


CHUNKS = 4


def level_tree(codes):
    rows = [jnp.float32(level) for level in nf4_levels]
    for bit in range(4):
        chosen = (codes & (1 << bit)) != 0
        rows = [jnp.where(chosen, rows[2 * n + 1], rows[2 * n]) for n in range(len(rows) // 2)]
    return rows[0]


def fused_kernel(
    fsdp,
    tensor,
    ids_any,
    live_any,
    owner_any,
    x_any,
    dv_any,
    code_any,
    scale_any,
    fd_any,
    fu_any,
    md_any,
    sd_any,
    mu_any,
    su_any,
    out_ref,
    nd_ref,
    nu_ref,
    nmd_ref,
    nsd_ref,
    nmu_ref,
    nsu_ref,
    ids_ref,
    live_ref,
    owner_ref,
    x_ref,
    dv_ref,
    code_ref,
    scale_ref,
    fd_ref,
    fu_ref,
    md_ref,
    sd_ref,
    mu_ref,
    su_ref,
    in_s,
    fac,
    gsend,
    gy,
    gz,
    grecv,
    dvs,
    part,
    col,
    wgt,
    outs,
    base,
    lows,
    fac_s,
    fac_f,
    fac_r,
    gy_s,
    gy_r,
    gz_s,
    gz_r,
    dvz_s,
    dvy_s,
    dvx_s,
    dvc_s,
    dv_r,
    part_s,
    part_r,
    col_s,
    col_r,
    wgt_s,
    wgt_r,
    out_s,
    out_r,
):
    f = lax.axis_index("fsdp")
    t = lax.axis_index("tensor")
    z, y = f // 2, f % 2
    x, c = t // 2, t % 2
    pair, odd = z // 2, z % 2
    wide, planes = tensor // 2, fsdp // 2
    tok_rows, width = x_ref.shape
    value = dv_ref.shape[1]
    w_rows = code_ref.shape[0]
    step_rows = w_rows // (2 * CHUNKS)
    rank = fd_ref.shape[1]
    slots = ids_ref.shape[0]
    seq = tok_rows // slots
    flat = fsdp * rank
    inverse_width = 1.0 / math.sqrt(MODEL_WIDTH)
    coefficient = adapter_scale / math.sqrt(ADAPTER_RANK)
    pending = []

    loads = {}
    for n, (name, src, dst) in enumerate(
        (
            ("fd", fd_any, fd_ref),
            ("fu", fu_any, fu_ref),
            ("dv", dv_any, dv_ref),
            ("live", live_any, live_ref),
            ("scale", scale_any, scale_ref),
            ("code", code_any, code_ref),
            ("x", x_any, x_ref),
            ("ids", ids_any, ids_ref),
            ("owner", owner_any, owner_ref),
            ("md", md_any, md_ref),
            ("sd", sd_any, sd_ref),
            ("mu", mu_any, mu_ref),
            ("su", su_any, su_ref),
        )
    ):
        loads[name] = pltpu.make_async_copy(src, dst, in_s.at[n])
        loads[name].start()

    def remote(src, dst, ss, rs, df, dt):
        return pltpu.make_async_remote_copy(
            src_ref=src,
            dst_ref=dst,
            send_sem=ss,
            recv_sem=rs,
            device_id={"fsdp": df, "tensor": dt},
            device_id_type=pl.DeviceIdType.MESH,
        )

    def send(copy, cond=None):
        if cond is None:
            copy.start()
        else:
            pl.when(cond)(copy.start)
        pending.append((copy, cond))

    barrier = pltpu.get_barrier_semaphore()
    greeted = []

    def greet(df, dt):
        pl.semaphore_signal(
            barrier,
            inc=1,
            device_id={"fsdp": df, "tensor": dt},
            device_id_type=pl.DeviceIdType.MESH,
        )
        greeted.append(1)

    for n in range(1, 8):
        near = 2 * pair + (odd + n // 4) % 2
        greet(2 * near + (y + n // 2) % 2, 2 * x + (c + n) % 2)
    for d in range(1, wide):
        for e in range(2):
            greet(2 * (2 * ((pair + d) % wide) + e) + y, t)
            greet(f, 2 * ((x + d) % wide) + e)

    loads["fd"].wait()
    loads["fu"].wait()
    fac[pl.ds(f, 1), :, 0:width] = fd_ref[...].astype(jnp.bfloat16)
    fac[pl.ds(f, 1), :, width : width + value] = fu_ref[...].astype(jnp.bfloat16)
    loads["dv"].wait()
    loads["live"].wait()
    tok_index = lax.broadcasted_iota(jnp.int32, (tok_rows, value), 0)
    masked = jnp.where(
        tok_index < live_ref[0] * seq, dv_ref[...].astype(jnp.float32), 0.0
    ).astype(jnp.bfloat16)
    dvs[t, odd, y] = masked

    def dequant(half, chunk):
        rows = pl.ds((half * CHUNKS + chunk) * step_rows, step_rows)
        levels = level_tree(code_ref[rows, :])
        scales = jnp.transpose(scale_ref[:, rows])
        blocks = scales.shape[1]
        block = value // blocks
        lane = lax.broadcasted_iota(jnp.int32, (step_rows, value), 1)
        spread = jnp.broadcast_to(scales[:, blocks - 1 : blocks], (step_rows, value))
        for n in reversed(range(blocks - 1)):
            spread = jnp.where(lane < (n + 1) * block, scales[:, n : n + 1], spread)
        col[pair, half, chunk] = (levels * spread).astype(jnp.bfloat16)

    pl.semaphore_wait(barrier, len(greeted))

    def fac_copy(dz, source):
        return remote(
            fac.at[source], fac.at[source], fac_s.at[dz], fac_r.at[source], (f + 2 * dz) % fsdp, t
        )

    def fac_forward(dz, source):
        return remote(
            fac.at[source], fac.at[source], fac_f.at[dz], fac_r.at[source], 2 * z + 1 - y, t
        )

    for dz in range(1, planes):
        send(fac_copy(dz, f))
    send(fac_forward(0, f))

    def dv_near(parity, sy):
        ref = dvs.at[t, parity, sy]
        return remote(ref, ref, dvz_s.at[0], dv_r.at[t, parity, sy], 2 * (4 * pair + 1 - z) + y, t)

    def dv_over(n, parity, sy):
        ref = dvs.at[t, parity, sy]
        return remote(ref, ref, dvy_s.at[n], dv_r.at[t, parity, sy], 2 * z + 1 - y, t)

    def dv_along(n, d, st, parity, sy):
        ref = dvs.at[st, parity, sy]
        to = 2 * ((x + d) % wide) + c
        return remote(ref, ref, dvx_s.at[n, d], dv_r.at[st, parity, sy], f, to)

    def dv_core(n, d, st, parity, sy):
        ref = dvs.at[st, parity, sy]
        return remote(ref, ref, dvc_s.at[n, d], dv_r.at[st, parity, sy], f, 2 * x + 1 - c)

    def dv_share(n, parity, sy):
        for d in range(1, wide):
            send(dv_along(n, d, t, parity, sy))
        send(dv_core(n, 0, t, parity, sy))

    send(dv_near(odd, y))
    send(dv_over(0, odd, y))
    dv_share(0, odd, y)

    def col_copy(d, source, half, chunk):
        ref = col.at[source, half, chunk]
        return remote(
            ref,
            ref,
            col_s.at[d, half, chunk],
            col_r.at[source, half, chunk],
            2 * (2 * ((pair + d) % wide) + odd) + y,
            t,
        )

    def wgt_copy(d, source, half, chunk):
        return remote(
            col.at[source, half, chunk],
            wgt.at[t, chunk],
            wgt_s.at[d, half, chunk],
            wgt_r.at[t, chunk],
            f,
            2 * source + half,
        )

    def hand_out(d, half, chunk):
        source = (pair + d) % wide
        send(wgt_copy(d, source, half, chunk), 2 * source + half != t)

    loads["scale"].wait()
    loads["code"].wait()
    for chunk in range(CHUNKS):
        for half in range(2):
            dequant(half, chunk)
            for d in range(1, wide):
                send(col_copy(d, pair, half, chunk))

    def forward(chunk):
        for d in range(1, wide):
            for half in range(2):
                col_copy(d, (pair + d) % wide, half, chunk).wait_recv()
                hand_out(d, half, chunk)

    def give(chunk):
        for half in range(2):
            hand_out(0, half, chunk)

    give(0)
    give(1)
    dv_over(0, odd, 1 - y).wait_recv()
    dv_share(1, odd, 1 - y)
    for later in range(2, CHUNKS):
        give(later)
    for dz in range(1, planes):
        source = (f + 2 * dz) % fsdp
        fac_copy(dz, source).wait_recv()
        send(fac_forward(dz, source))
    dv_near(1 - odd, y).wait_recv()
    send(dv_over(1, 1 - odd, y))
    dv_share(2, 1 - odd, y)
    dv_over(1, 1 - odd, 1 - y).wait_recv()
    dv_share(3, 1 - odd, 1 - y)

    loads["ids"].wait()
    loads["owner"].wait()
    slot_row = jnp.zeros((1, tok_rows), jnp.int32)
    seq_row = lax.broadcasted_iota(jnp.int32, (1, tok_rows), 1) // seq
    for n in range(slots):
        own = jnp.int32(0)
        for u in range(fsdp):
            own = own + jnp.where(ids_ref[n] == u, owner_ref[u], 0)
        slot_row = jnp.where(seq_row == n, own, slot_row)
    named = lax.broadcasted_iota(jnp.int32, (flat, tok_rows), 0) // rank
    chosen = named == jnp.broadcast_to(slot_row, (flat, tok_rows))

    forward(0)
    for dz in range(planes):
        source = (2 * z + 2 * dz) % fsdp + 1 - y
        fac_forward(dz, source).wait_recv()
    loads["x"].wait()
    all_down = fac[:, :, 0:width].reshape(flat, width)
    all_up = fac[:, :, width : width + value].reshape(flat, value)

    def folded(scores, factor):
        kept = jnp.where(chosen, scores, 0.0).reshape(fsdp, rank, tok_rows)
        return jnp.sum(kept, axis=0) * factor

    part[t, 0:rank, :] = folded(right_product(all_down, x_ref[...]), inverse_width)
    part[t, rank : 2 * rank, :] = folded(right_product(all_up, masked), coefficient)

    def part_copy(dt, source):
        return remote(part.at[source], part.at[source], part_s.at[dt], part_r.at[source], f, dt)

    for step in range(1, tensor):
        send(part_copy((t + step) % tensor, t))

    for n, (parity, sy) in enumerate(
        ((odd, y), (odd, 1 - y), (1 - odd, y), (1 - odd, 1 - y))
    ):
        for d in range(1, wide):
            st = 2 * ((x + d) % wide) + c
            dv_along(n, d, st, parity, sy).wait_recv()
            send(dv_core(n, d, st, parity, sy))
    forward(1)

    for d in range(wide):
        for parity in range(2):
            for sy in range(2):
                dv_core(0, 0, 2 * d + 1 - c, parity, sy).wait_recv()

    def multiply(chunk):
        for step in range(1, tensor):
            source = (t + step) % tensor
            arrived = remote(
                col.at[0, 0, chunk],
                wgt.at[source, chunk],
                wgt_s.at[0, 0, chunk],
                wgt_r.at[source, chunk],
                f,
                source,
            )
            arrived.wait_recv()
        rows = 4 * tok_rows
        total = right_product(dvs[t].reshape(rows, value), col[x, c, chunk])
        for step in range(1, tensor):
            source = (t + step) % tensor
            total = total + right_product(dvs[source].reshape(rows, value), wgt[source, chunk])
        for parity in range(2):
            for half in range(2):
                start = (2 * parity + half) * tok_rows
                piece = total[start : start + tok_rows].astype(jnp.bfloat16)
                outs[chunk, parity, half] = piece
                df, dt = 2 * (2 * pair + parity) + half, 2 * x + odd
                stays = jnp.logical_and(df == f, dt == t)

                @pl.when(stays)
                def _(piece=piece):
                    base[y, c, chunk] = piece

                copy = remote(
                    outs.at[chunk, parity, half],
                    base.at[y, c, chunk],
                    out_s.at[chunk, parity, half],
                    out_r.at[y, c, chunk],
                    df,
                    dt,
                )
                send(copy, jnp.logical_not(stays))

    multiply(0)

    for step in range(1, tensor):
        source = (t + step) % tensor
        part_copy(source, source).wait_recv()
    sums = jnp.sum(part[...], axis=0)
    low = sums.astype(jnp.bfloat16).astype(jnp.float32)

    def spread_out(rows):
        tiled = jnp.broadcast_to(rows[None], (fsdp, rank, tok_rows)).reshape(flat, tok_rows)
        return jnp.where(chosen, tiled, 0.0).astype(jnp.bfloat16)

    in_spread = spread_out(low[0:rank])
    grad_spread = spread_out(low[rank : 2 * rank])
    down_terms = jnp.dot(grad_spread, x_ref[...], preferred_element_type=jnp.float32)
    by_slot = (down_terms * inverse_width).astype(jnp.bfloat16).reshape(fsdp, rank, width)
    up_terms = jnp.dot(in_spread, masked, preferred_element_type=jnp.float32)
    up_slot = (up_terms * coefficient).astype(jnp.bfloat16).reshape(fsdp, rank, value)
    for slot in range(fsdp):
        gsend[slot % 2, slot // 2, :, 0:width] = by_slot[slot]
        gsend[slot % 2, slot // 2, :, width : width + value] = up_slot[slot]
    over = remote(gsend.at[1 - y], gy, gy_s.at[0], gy_r.at[0], 2 * z + 1 - y, t)
    send(over)

    def grad_copy(dz, to, source):
        return remote(
            gz.at[to], grecv.at[source], gz_s.at[dz], gz_r.at[source], (f + 2 * dz) % fsdp, t
        )

    multiply(1)
    forward(2)
    over.wait_recv()
    gz[...] = (gsend[y].astype(jnp.float32) + gy[...].astype(jnp.float32)).astype(jnp.bfloat16)
    for dz in range(1, planes):
        send(grad_copy(dz, (z + dz) % planes, z))
    grecv[pl.ds(z, 1)] = gz[pl.ds(z, 1)]
    multiply(2)
    lows[...] = inverse_width * lax.dot_general(
        grad_spread, all_down, (((0,), (0,)), ((), ())), preferred_element_type=jnp.float32
    )
    for later in range(3, CHUNKS):
        forward(later)
        multiply(later)

    def finish(chunk):
        for half in range(2):
            for core in range(2):
                stays = jnp.logical_and(odd == c, jnp.logical_and(half == y, core == c))
                arrived = remote(
                    outs.at[chunk, 0, 0],
                    base.at[half, core, chunk],
                    out_s.at[chunk, 0, 0],
                    out_r.at[half, core, chunk],
                    f,
                    2 * x + 1 - c,
                )
                pl.when(jnp.logical_not(stays))(arrived.wait_recv)
                start = half * w_rows + (core * CHUNKS + chunk) * step_rows
                stop = start + step_rows
                out_ref[:, start:stop] = (
                    base[half, core, chunk].astype(jnp.float32) + lows[:, start:stop]
                ).astype(jnp.bfloat16)

    for chunk in range(CHUNKS - 1):
        finish(chunk)
    for dz in range(1, planes):
        grad_copy(dz, 0, (z + dz) % planes).wait_recv()
    for name in ("md", "sd", "mu", "su"):
        loads[name].wait()
    down_grad = jnp.sum(grecv[:, :, 0:width].astype(jnp.float32), axis=0, keepdims=True)
    up_grad = jnp.sum(
        grecv[:, :, width : width + value].astype(jnp.float32), axis=0, keepdims=True
    )
    nd_ref[...], nmd_ref[...], nsd_ref[...] = adam_update(
        fd_ref[...], down_grad, md_ref[...], sd_ref[...]
    )
    nu_ref[...], nmu_ref[...], nsu_ref[...] = adam_update(
        fu_ref[...], up_grad, mu_ref[...], su_ref[...]
    )

    finish(CHUNKS - 1)

    for copy, cond in pending:
        if cond is None:
            copy.wait_send()
        else:
            pl.when(cond)(copy.wait_send)


def write_kernel(count, *refs):
    held, sems = refs[2 * count : 3 * count], refs[3 * count]
    loads = [pltpu.make_async_copy(refs[n], held[n], sems.at[0, n]) for n in range(count)]
    stores = [pltpu.make_async_copy(held[n], refs[count + n], sems.at[1, n]) for n in range(count)]
    for load in loads:
        load.start()
    for load, store in zip(loads, stores):
        load.wait()
        store.start()
    for store in stores:
        store.wait()


def fused(fsdp, tensor, *args):
    (
        layer_input,
        value_grad,
        quant_codes,
        block_scales,
        tenant_ids,
        live_counts,
        tenant_owner,
        factor_down,
        factor_up,
        moment_down,
        second_down,
        moment_up,
        second_up,
    ) = args
    tok_rows, width = layer_input.shape
    value = value_grad.shape[1]
    w_rows = quant_codes.shape[0]
    rank = factor_down.shape[1]
    step_rows = w_rows // (2 * CHUNKS)
    wide, planes = tensor // 2, fsdp // 2
    low = jnp.bfloat16
    dma = pltpu.SemaphoreType.DMA
    vmem = pl.BlockSpec(memory_space=pltpu.VMEM)
    like = jax.ShapeDtypeStruct
    shapes = (
        like(layer_input.shape, low),
        like(factor_down.shape, jnp.float32),
        like(factor_up.shape, jnp.float32),
        like(factor_down.shape, jnp.float32),
        like(factor_down.shape, jnp.float32),
        like(factor_up.shape, jnp.float32),
        like(factor_up.shape, jnp.float32),
    )
    anywhere = pl.BlockSpec(memory_space=pl.ANY)
    results = pl.pallas_call(
        functools.partial(fused_kernel, fsdp, tensor),
        out_shape=shapes,
        in_specs=[anywhere] * 13,
        out_specs=(vmem,) * 7,
        scratch_shapes=[
            pltpu.SMEM(tenant_ids.shape, jnp.int32),
            pltpu.SMEM(live_counts.shape, jnp.int32),
            pltpu.SMEM(tenant_owner.shape, jnp.int32),
            pltpu.VMEM(layer_input.shape, low),
            pltpu.VMEM(value_grad.shape, low),
            pltpu.VMEM(quant_codes.shape, jnp.int32),
            pltpu.VMEM(block_scales.shape[::-1], jnp.float32),
            pltpu.VMEM(factor_down.shape, jnp.float32),
            pltpu.VMEM(factor_up.shape, jnp.float32),
            pltpu.VMEM(moment_down.shape, jnp.float32),
            pltpu.VMEM(second_down.shape, jnp.float32),
            pltpu.VMEM(moment_up.shape, jnp.float32),
            pltpu.VMEM(second_up.shape, jnp.float32),
            dma((13,)),
            pltpu.VMEM((fsdp, rank, width + value), low),
            pltpu.VMEM((2, planes, rank, width + value), low),
            pltpu.VMEM((planes, rank, width + value), low),
            pltpu.VMEM((planes, rank, width + value), low),
            pltpu.VMEM((planes, rank, width + value), low),
            pltpu.VMEM((tensor, 2, 2, tok_rows, value), low),
            pltpu.VMEM((tensor, 2 * rank, tok_rows), jnp.float32),
            pltpu.VMEM((wide, 2, CHUNKS, step_rows, value), low),
            pltpu.VMEM((tensor, CHUNKS, step_rows, value), low),
            pltpu.VMEM((CHUNKS, 2, 2, tok_rows, step_rows), low),
            pltpu.VMEM((2, 2, CHUNKS, tok_rows, step_rows), low),
            pltpu.VMEM((tok_rows, width), jnp.float32),
            dma((planes,)),
            dma((planes,)),
            dma((fsdp,)),
            dma((1,)),
            dma((1,)),
            dma((planes,)),
            dma((planes,)),
            dma((1,)),
            dma((2,)),
            dma((4, wide)),
            dma((4, wide)),
            dma((tensor, 2, 2)),
            dma((tensor,)),
            dma((tensor,)),
            dma((wide, 2, CHUNKS)),
            dma((wide, 2, CHUNKS)),
            dma((wide, 2, CHUNKS)),
            dma((tensor, CHUNKS)),
            dma((CHUNKS, 2, 2)),
            dma((2, 2, CHUNKS)),
        ],
        compiler_params=pltpu.CompilerParams(
            collective_id=0, has_side_effects=True, vmem_limit_bytes=60 * 1024 * 1024
        ),
    )(
        tenant_ids,
        live_counts,
        tenant_owner,
        layer_input,
        value_grad,
        quant_codes,
        block_scales.T,
        factor_down,
        factor_up,
        moment_down,
        second_down,
        moment_up,
        second_up,
    )
    return pl.pallas_call(
        functools.partial(write_kernel, len(shapes)),
        out_shape=shapes,
        in_specs=[anywhere] * len(shapes),
        out_specs=(anywhere,) * len(shapes),
        scratch_shapes=[pltpu.VMEM(s.shape, s.dtype) for s in shapes] + [dma((2, len(shapes)))],
        compiler_params=pltpu.CompilerParams(vmem_limit_bytes=60 * 1024 * 1024),
    )(*results)


def solution(mesh):
    fsdp, tensor = mesh.shape["fsdp"], mesh.shape["tensor"]
    planar = fsdp == 2 * tensor and tensor % 2 == 0
    body = functools.partial(fused, fsdp, tensor) if planar else shards
    in_specs = (
        P("fsdp", "tensor"),
        P("fsdp", "tensor"),
        P("fsdp", "tensor"),
        P("fsdp", "tensor"),
        P("fsdp"),
        P("fsdp"),
        P(),
        P("fsdp", None, "tensor"),
        P("fsdp", None, "tensor"),
        P("fsdp", None, "tensor"),
        P("fsdp", None, "tensor"),
        P("fsdp", None, "tensor"),
        P("fsdp", None, "tensor"),
    )
    out_specs = (
        P("fsdp", "tensor"),
        P("fsdp", None, "tensor"),
        P("fsdp", None, "tensor"),
        P("fsdp", None, "tensor"),
        P("fsdp", None, "tensor"),
        P("fsdp", None, "tensor"),
        P("fsdp", None, "tensor"),
    )
    return jax.shard_map(body, mesh=mesh, in_specs=in_specs, out_specs=out_specs, check_vma=False)
```
